256 devices in a mesh: ctx: 16 (over x, y_hi, core), head: 16 (over z, y_lo).
Axes of the slice: x: 4, y: 4 (y_hi: 2, y_lo: 2; y = y_hi * 2 + y_lo), z: 8, core: 2. Of those that a mesh axis runs over, the one named last changes fastest.
Arguments:
- latent: bfloat16 [2048, 576], P('ctx'), may hold values from -6 to 6
- query: bfloat16 [2048, 12288], P('ctx', 'head'), may hold values from -20 to 20
- up_key: bfloat16 [512, 8192], P(None, 'head'), may hold values from -0.25 to 0.25
- up_value: bfloat16 [512, 8192], P(None, 'head'), may hold values from -1 to 1
- out_grad: bfloat16 [2048, 8192], P('ctx', 'head'), may hold values from -6 to 6
- block_pos: int32 [32], replicated, may hold values from 0 to 31, each once
Outputs:
- attention_out: bfloat16 [2048, 8192], P('ctx', 'head')
- query_grad: bfloat16 [2048, 12288], P('ctx', 'head')
- latent_grad: float32 [2048, 576], P(('ctx', 'head'))
- up_key_grad: float32 [512, 8192], P('ctx', 'head')
- up_value_grad: float32 [512, 8192], P('ctx', 'head')
The draws below stay inside these ranges and needn't reach their ends.
Inputs may be any that keep to these rules, and one draw needn't show every extreme that they name: `block_pos`: every half-block position appears exactly once.
All inputs are finite; a program needn't handle non-finite values.
Results may differ from the reference program's by a relative error of at most 0.035.
Values may be sent and summed in bfloat16 or wider, within the bound.
A program may use at most 64 MiB of HBM per device.

```python
import math
import jax
import jax.numpy as jnp
from jax import lax

LATENT = 512
ROPE = 64
NOPE = 128
VDIM = 128
HEADS = 64
TOK_DEV = 128
SEQ = 2048
N_CTX = 16


def shared_rope(key):
    seq_rows = TOK_DEV * N_CTX
    gauss = jax.random.normal(jax.random.fold_in(key, 11), (seq_rows, ROPE), jnp.float32)
    return gauss


def draw_latent(key, part):
    gauss = shared_rope(key)
    key = jax.random.fold_in(key, 1)
    seq_rows = TOK_DEV * N_CTX
    nope_part = jnp.clip(jax.random.normal(key, (seq_rows, LATENT), jnp.float32), -6.0, 6.0)
    rope_part = jnp.clip(gauss, -6.0, 6.0)
    return jnp.concatenate([nope_part, rope_part], 1).astype(jnp.bfloat16)


def draw_query(key, part):
    key = jax.random.fold_in(key, 2)
    seq_rows = TOK_DEV * N_CTX
    whole = jnp.clip(jax.random.normal(key, (seq_rows, HEADS, NOPE + ROPE), jnp.float32), -6.0, 6.0)
    return whole.reshape(seq_rows, HEADS * (NOPE + ROPE)).astype(jnp.bfloat16)


def spiked(values, rng, source, target, parts, factor):
    owner, partner = [(jnp.arange(values.shape[dim]) // (values.shape[dim] // parts)).reshape([-1 if axis == dim else 1 for axis in range(values.ndim)]) for dim in (source, target)]
    chosen = jax.random.permutation(rng, parts)[partner]
    strong = (owner == chosen) | (owner == (partner + parts // 2) % parts)
    return jnp.where(strong, factor * values, values)


def level_of(stream_key, dims, pieces, least, largest):
    def one(dim, shards_of):
        steps = jax.random.uniform(jax.random.fold_in(jax.random.fold_in(stream_key, 6), dim), (shards_of,), jnp.float32, least / len(pieces), largest / len(pieces))
        return jnp.repeat(jnp.exp(steps), dims[dim] // shards_of).reshape((-1,) + (1,) * (len(dims) - dim - 1))

    gain = one(*pieces[0])
    for cut in pieces[1:]:
        gain = gain * one(*cut)
    return gain


def bell_draw(stream_key, dims, deviation, most, pieces=(), kind=jnp.bfloat16):
    drawn = jax.random.normal(stream_key, dims, jnp.float32) * deviation
    if len(pieces) > 0:
        drawn = level_of(stream_key, dims, pieces, -0.22, 0.18) * drawn
    return jnp.clip(drawn, min=-most, max=most).astype(kind)


def noise_with(own_key, dims, scale, limit, pieces, heavy, kind=jnp.bfloat16):
    drawn = scale * jax.random.normal(own_key, dims, jnp.float32)
    if pieces:
        drawn = drawn * level_of(own_key, dims, pieces, -0.22, 0.18)
    return jnp.clip(spiked(drawn, jax.random.fold_in(own_key, 3), *heavy), -limit, limit).astype(kind)


def setup_inputs(seed: int = 0) -> dict:
    key_of = jax.random.split(jax.random.key(seed), 7)
    latent = draw_latent(jax.random.fold_in(key_of[6], 71), 0)
    query = draw_query(jax.random.fold_in(key_of[6], 71), 0)
    up_key = bell_draw(key_of[2], (LATENT, HEADS * NOPE), LATENT ** -0.5, 0.25, ((1, 16),))
    up_value = bell_draw(key_of[3], (LATENT, HEADS * VDIM), (LATENT // 16) ** -0.5, 1.0, ((1, 16),))
    out_grad = noise_with(key_of[4], (SEQ, HEADS * VDIM), 1.0, 6.0, ((0, 16), (1, 16)), (1, 0, 16, 2.0))
    block_pos = jax.random.permutation(key_of[5], 2 * N_CTX).astype(jnp.int32)
    return {"latent": latent, "query": query, "up_key": up_key, "up_value": up_value, "out_grad": out_grad, "block_pos": block_pos}


def token_positions(row_ids, block_pos, half_rows):
    return jnp.take(block_pos, row_ids // half_rows).astype(jnp.int32) * half_rows + row_ids % half_rows

def reference(latent, query, up_key, up_value, out_grad, block_pos):
    seq_rows = latent.shape[0]
    qk_width = NOPE + ROPE
    score_scale = 1.0 / math.sqrt(qk_width)
    row_ids = jnp.arange(seq_rows, dtype=jnp.int32)
    position = token_positions(row_ids, block_pos, TOK_DEV // 2)
    visible = position[:, None] >= position[None, :]
    nope_part = latent[:, :LATENT]
    rope_part = latent[:, LATENT:]
    highest = lax.Precision.HIGHEST
    blocks = seq_rows // TOK_DEV
    nope_tiled = jnp.tile(nope_part.T, (1, blocks))

    def one_head(lat_grad, index_head):
        key_weight = lax.dynamic_slice_in_dim(up_key, index_head * NOPE, NOPE, 1)
        value_weight = lax.dynamic_slice_in_dim(up_value, index_head * VDIM, VDIM, 1)
        query_rows = lax.dynamic_slice_in_dim(query, index_head * qk_width, qk_width, 1)
        grad_rows = lax.dynamic_slice_in_dim(out_grad, index_head * VDIM, VDIM, 1)
        key_nope = jnp.dot(nope_part, key_weight, preferred_element_type=jnp.float32).astype(jnp.bfloat16)
        value_rows = jnp.dot(nope_part, value_weight, preferred_element_type=jnp.float32).astype(jnp.bfloat16)
        key_rows = jnp.concatenate([key_nope, rope_part], 1)
        logits = jnp.dot(query_rows, key_rows.T, preferred_element_type=jnp.float32) * score_scale
        logits = jnp.where(visible, logits, jnp.float32(-jnp.inf))
        row_max = lax.optimization_barrier(jnp.max(logits, axis=1))
        expo = jnp.exp(logits - row_max[:, None])
        row_sum = lax.optimization_barrier(jnp.sum(expo, axis=1))
        output = (jnp.dot(expo.astype(jnp.bfloat16), value_rows, preferred_element_type=jnp.float32) / row_sum[:, None]).astype(jnp.bfloat16)
        log_total = row_max + jnp.log(row_sum)
        prob = jnp.exp(logits - log_total[:, None])
        prob_low = prob.astype(jnp.bfloat16)
        prob_blocks = prob_low.astype(jnp.float32).reshape(blocks, TOK_DEV, seq_rows)
        grad_blocks = grad_rows.astype(jnp.float32).reshape(blocks, TOK_DEV, VDIM)
        value_parts = jnp.einsum('cqk,cqd->ckd', prob_blocks, grad_blocks, precision=highest).astype(jnp.bfloat16)
        prob_grad = jnp.dot(grad_rows, value_rows.T, preferred_element_type=jnp.float32)
        row_delta = lax.optimization_barrier(jnp.sum(grad_rows.astype(jnp.float32) * output.astype(jnp.float32), axis=1))
        score_grad = (prob * (prob_grad - row_delta[:, None])).astype(jnp.bfloat16)
        query_part = (jnp.dot(score_grad, key_rows, preferred_element_type=jnp.float32) * score_scale).astype(jnp.bfloat16)
        score_blocks = score_grad.astype(jnp.float32).reshape(blocks, TOK_DEV, seq_rows)
        query_blocks = query_rows.astype(jnp.float32).reshape(blocks, TOK_DEV, qk_width)
        key_parts = jnp.einsum('cqk,cqd->ckd', score_blocks, query_blocks, precision=highest) * score_scale
        key_nope_parts = key_parts[:, :, :NOPE].astype(jnp.bfloat16)
        rope_grad = lax.optimization_barrier(jnp.sum(key_parts[:, :, NOPE:], axis=0))
        nope_flat = key_nope_parts.transpose(1, 0, 2).reshape(seq_rows, blocks * NOPE)
        value_flat = value_parts.transpose(1, 0, 2).reshape(seq_rows, blocks * VDIM)
        nope_grad = jnp.dot(nope_flat, jnp.tile(key_weight.T, (blocks, 1)), preferred_element_type=jnp.float32)
        nope_grad = nope_grad + jnp.dot(value_flat, jnp.tile(value_weight.T, (blocks, 1)), preferred_element_type=jnp.float32)
        lat_grad = lat_grad + jnp.concatenate([nope_grad, rope_grad], 1)
        key_weight_grad = jnp.dot(nope_tiled, key_nope_parts.reshape(blocks * seq_rows, NOPE), preferred_element_type=jnp.float32)
        value_weight_grad = jnp.dot(nope_tiled, value_parts.reshape(blocks * seq_rows, VDIM), preferred_element_type=jnp.float32)
        return (lat_grad, (output, query_part, key_weight_grad, value_weight_grad))
    start_grad = jnp.zeros((seq_rows, LATENT + ROPE), jnp.float32)
    lat_grad, stacked = lax.scan(one_head, start_grad, jnp.arange(HEADS, dtype=jnp.int32))
    outputs, query_parts, key_grads, value_grads = stacked
    attention_out = outputs.transpose(1, 0, 2).reshape(seq_rows, HEADS * VDIM)
    query_grad = query_parts.transpose(1, 0, 2).reshape(seq_rows, HEADS * qk_width)
    up_key_grad = key_grads.transpose(1, 0, 2).reshape(LATENT, HEADS * NOPE)
    up_value_grad = value_grads.transpose(1, 0, 2).reshape(LATENT, HEADS * VDIM)
    return (attention_out, query_grad, lat_grad, up_key_grad, up_value_grad)
```

```python
import functools
import math

import jax
import jax.numpy as jnp
from jax import lax
from jax.experimental import pallas as pl
from jax.experimental.pallas import tpu as pltpu
from jax.sharding import PartitionSpec as P

LATENT = 512
ROPE = 64
WIDTH = LATENT + ROPE
NOPE = 128
VDIM = 128
QK = NOPE + ROPE
ROWS = 128
HEADS_DEV = 4
STACK = HEADS_DEV * ROWS
SEQ = 2048
SCALE = 1.0 / math.sqrt(QK)
LOG2E = 1.4426950408889634
MASKED = -1e30

BF = jnp.bfloat16
F32 = jnp.float32


def dot(a, b):
    return jnp.dot(a, b, preferred_element_type=F32)


def flip(a):
    return a.astype(F32).T


def slot(i, dk, dy):
    return i * 4 + dk * 2 + dy


def other(a, flip_it):
    return 1 - a if flip_it else a


def kernel(
    latent_t_hbm, query_hbm, wk_hbm, wv_hbm, dout_hbm, bpos,
    out_ref, dq_ref, dlat_ref, dwk_ref, dwv_ref,
    lat, lat_t, q_v, wk, wv, do_v, wk_t, wv_t, q_t, do_t, q_nope,
    qs_t, qd, q_rope, dlift, dos_t, scores, ed, lift_acc, lift_t, o_t, dq_t, dql,
    top, delta_row, part, r_sib, x_first, r_x1, a_1, r_y1, y_first, r_y2, a_2, r_x2,
    to_z, r_z, w_own, w_sib, w_acc, w_r,
    load_sem, send_sem, recv_sem,
):
    ctx, head = lax.axis_index("ctx"), lax.axis_index("head")
    x, yh, core = lax.div(ctx, 4), lax.rem(lax.div(ctx, 2), 2), lax.rem(ctx, 2)
    z, yl = lax.div(head, 2), lax.rem(head, 2)

    def x_at(i):
        return lax.rem(x + i, 4)

    def dev(i, dy, dk, dz, dl):
        xx, yy, kk = x_at(i), other(yh, dy), other(core, dk)
        return ((xx * 2 + yy) * 2 + kk, lax.rem(z + dz, 8) * 2 + other(yl, dl))

    sib = dev(0, 0, 1, 0, 0)
    near_y = dev(0, 1, 0, 0, 1)
    along_x = [None] + [dev(i, 0, 0, 0, 0) for i in range(1, 4)]
    y_steps = [(0, 1), (1, 0), (1, 1)]
    along_y = [dev(0, dy, 0, 0, dl) for dy, dl in y_steps]
    along_z = [dev(0, 0, 0, d, 0) for d in range(1, 8)]
    plane_steps = [(i, dy) for i in range(4) for dy in range(2)][1:]
    plane = [dev(i, dy, 0, 0, 0) for i, dy in plane_steps]

    loads = [
        pltpu.make_async_copy(src, dst, load_sem.at[n])
        for n, (src, dst) in enumerate(
            [
                (latent_t_hbm, lat_t.at[0]),
                (query_hbm, q_v),
                (wk_hbm, wk),
                (dout_hbm, do_v),
                (wv_hbm, wv),
            ]
        )
    ]
    for load in loads:
        load.start()

    barrier = pltpu.get_barrier_semaphore()
    partners = [sib] + plane + [along_y[0], along_y[2]] + along_z
    for partner in partners:
        pl.semaphore_signal(barrier, inc=1, device_id=partner, device_id_type=pl.DeviceIdType.MESH)
    pl.semaphore_wait(barrier, len(partners))

    started = []

    def send(src, dst, to):
        n = len(started)
        copy = pltpu.make_async_remote_copy(
            src_ref=src, dst_ref=dst, send_sem=send_sem.at[n], recv_sem=recv_sem.at[n],
            device_id=to, device_id_type=pl.DeviceIdType.MESH,
        )
        copy.start()
        started.append(copy)
        return copy

    def block(i, dk, dy):
        return lat_t.at[slot(i, dk, dy)]

    def pass_on(i, dy):
        return send(block(i, 0, dy), block(i, 1, dy), sib)

    loads[0].wait()
    own = lat_t.at[0]
    from_x2 = send(own, block(2, 0, 0), along_x[2])
    from_y = send(own, block(0, 0, 1), near_y)
    from_x3 = send(own, block(3, 0, 0), along_x[1])
    from_x1 = send(own, block(1, 0, 0), along_x[3])
    sib_got = {(0, 0): pass_on(0, 0)}

    for load in loads[1:]:
        load.wait()

    def lift_queries():
        q_t[...] = flip(q_v[...]).astype(BF)
        do_t[...] = flip(do_v[...]).astype(BF)
        for h in range(HEADS_DEV):
            cols = slice(h * ROWS, (h + 1) * ROWS)
            q_h_t = q_t[h * QK : h * QK + NOPE, :]
            q_lift = dot(wk[:, cols], q_h_t)
            qs_t[:LATENT, cols] = (q_lift * (SCALE * LOG2E)).astype(BF)
            rope_t = q_t[h * QK + NOPE : (h + 1) * QK, :].astype(F32)
            qs_t[LATENT:, cols] = (rope_t * (SCALE * LOG2E)).astype(BF)

    lift_queries()
    query_row = lax.broadcasted_iota(jnp.int32, (1, STACK), 1)
    query_pos = (
        jnp.where(lax.rem(query_row, 128) < 64, bpos[2 * ctx], bpos[2 * ctx + 1]) * 64
        + lax.rem(query_row, 64)
    )
    top[...] = jnp.full(top.shape, MASKED, F32)
    key_row = lax.broadcasted_iota(jnp.int32, (ROWS, 1), 0)

    def score_block(i, dk, dy):
        rows = pl.ds(slot(i, dk, dy) * ROWS, ROWS)
        owner = (x_at(i) * 2 + other(yh, dy)) * 2 + other(core, dk)
        keys = flip(lat_t[slot(i, dk, dy)]).astype(BF)
        lat[rows, :] = keys
        key_pos = (
            jnp.where(key_row < 64, bpos[2 * owner], bpos[2 * owner + 1]) * 64
            + lax.rem(key_row, 64)
        )
        s = jnp.where(key_pos <= query_pos, dot(keys, qs_t[...]), MASKED)
        scores[rows, :] = s
        top[...] = jnp.maximum(top[...], jnp.max(s.reshape(ROWS // 8, 8, STACK), axis=0))

    score_block(0, 0, 0)
    from_y.wait_recv()
    up_x3 = send(block(0, 0, 1), block(3, 0, 1), along_x[1])
    up_x1 = send(block(0, 0, 1), block(1, 0, 1), along_x[3])
    sib_got[0, 1] = pass_on(0, 1)
    sib_got[0, 0].wait_recv()
    score_block(0, 1, 0)
    from_x2.wait_recv()
    up_y = send(block(2, 0, 0), block(2, 0, 1), near_y)
    sib_got[2, 0] = pass_on(2, 0)
    from_x3.wait_recv()
    sib_got[3, 0] = pass_on(3, 0)
    from_x1.wait_recv()
    sib_got[1, 0] = pass_on(1, 0)
    score_block(0, 0, 1)
    score_block(2, 0, 0)
    score_block(3, 0, 0)
    score_block(1, 0, 0)

    def lift_rest():
        wk_t[...] = flip(wk[...]).astype(BF)
        wv_t[...] = flip(wv[...]).astype(BF)
        for h in range(HEADS_DEV):
            cols = slice(h * ROWS, (h + 1) * ROWS)
            q_nope[:, cols] = flip(q_t[h * QK : h * QK + NOPE, :]).astype(BF)
            rope = flip(q_t[h * QK + NOPE : (h + 1) * QK, :])
            q_rope[cols, :] = (rope * SCALE).astype(BF)
            qd[cols, :] = (dot(q_nope[:, cols], wk_t[cols, :]) * SCALE).astype(BF)
            dlift[:, cols] = dot(wv[:, cols], do_t[cols, :])

    lift_rest()
    sib_got[0, 1].wait_recv()
    score_block(0, 1, 1)
    sib_got[2, 0].wait_recv()
    score_block(2, 1, 0)
    up_x3.wait_recv()
    sib_got[3, 1] = pass_on(3, 1)
    up_x1.wait_recv()
    sib_got[1, 1] = pass_on(1, 1)
    sib_got[3, 0].wait_recv()
    score_block(3, 1, 0)
    sib_got[1, 0].wait_recv()
    score_block(1, 1, 0)
    up_y.wait_recv()
    sib_got[2, 1] = pass_on(2, 1)
    score_block(3, 0, 1)
    score_block(1, 0, 1)
    score_block(2, 0, 1)
    sib_got[3, 1].wait_recv()
    score_block(3, 1, 1)
    sib_got[1, 1].wait_recv()
    score_block(1, 1, 1)
    sib_got[2, 1].wait_recv()
    score_block(2, 1, 1)

    def four(c, width):
        return jnp.concatenate([lat_t[c * 4 + n, :width, :] for n in range(4)], axis=1)

    def forward():
        row_max = jnp.max(top[...], axis=0, keepdims=True)
        total = jnp.zeros((8, STACK), F32)
        for c in range(4):
            rows = slice(c * 512, (c + 1) * 512)
            e = jnp.exp2(scores[rows, :] - row_max)
            total = total + jnp.sum(e.reshape(64, 8, STACK), axis=0)
            ed[rows, STACK:] = e.astype(BF)
            add = dot(four(c, LATENT), ed[rows, STACK:])
            if c == 0:
                lift_acc[...] = add
            else:
                lift_acc[...] += add
        inverse = 1.0 / jnp.sum(total, axis=0, keepdims=True)
        lift_t[...] = (lift_acc[...] * inverse).astype(BF)
        deltas = []
        for h in range(HEADS_DEV):
            cols = slice(h * ROWS, (h + 1) * ROWS)
            o_low = dot(wv_t[cols, :], lift_t[:, cols]).astype(BF)
            o_t[cols, :] = o_low
            deltas.append(
                jnp.sum(do_t[cols, :].astype(F32) * o_low.astype(F32), axis=0, keepdims=True)
            )
            scaled = dlift[:, cols] * inverse[:, cols]
            dos_t[:, cols] = scaled.astype(BF)
            qd[STACK + h * ROWS : STACK + (h + 1) * ROWS, :] = scaled.T.astype(BF)
        delta_row[...] = jnp.concatenate(deltas, axis=1) * inverse

    forward()

    def weight_terms(n, lifted, by):
        for h in range(HEADS_DEV):
            cols = slice(h * ROWS, (h + 1) * ROWS)
            g = dot(lifted[:, cols], by[:, cols]).astype(BF)
            for piece in range(16):
                w_own[n, piece % 2, piece // 2, :, cols] = g[piece * 32 : (piece + 1) * 32, :]
        return send(w_own.at[n, 1 - core], w_sib.at[n], sib)

    def weight_sends(n, arrived):
        arrived.wait_recv()
        w_acc[n] = (w_own[n, core].astype(F32) + w_sib[n].astype(F32)).astype(BF)
        return [
            send(w_acc.at[n, x_at(i) * 2 + other(yh, dy)], w_r.at[n, m], plane[m])
            for m, (i, dy) in enumerate(plane_steps)
        ]

    def weight_end(n, arrived, ref):
        total = w_acc[n, x * 2 + yh].astype(F32)
        for m, copy in enumerate(arrived):
            copy.wait_recv()
            total = total + w_r[n, m].astype(F32)
        ref[...] = total

    def unit(i, dk):
        u = i * 2 + dk
        rows = slice(u * 256, (u + 1) * 256)
        dp = dot(lat[rows, :LATENT], dos_t[...])
        ds = (ed[rows, STACK:].astype(F32) * (dp - delta_row[...])).astype(BF)
        ed[rows, :STACK] = ds
        nope = dot(ed[rows, :], qd[...])
        rope = dot(ds, q_rope[...])
        for half in range(2):
            for dy in range(2):
                for low in range(2):
                    starts = [dy * 128 + half * 64 + n * 16 + low * 8 for n in range(4)]
                    part[u, half, dy, low, :, :LATENT] = jnp.concatenate(
                        [nope[r : r + 8, :] for r in starts], axis=0
                    ).astype(BF)
                    part[u, half, dy, low, :, LATENT:] = jnp.concatenate(
                        [rope[r : r + 8, :] for r in starts], axis=0
                    ).astype(BF)

    def to_sib(i):
        return send(part.at[i * 2 + 1], r_sib.at[i], sib)

    def on_chip(i, arrived):
        arrived.wait_recv()
        x_first[i] = (part[i * 2, 0].astype(F32) + r_sib[i, 0].astype(F32)).astype(BF)
        copy = send(x_first.at[i], r_x1.at[i - 1], along_x[i]) if i else None
        y_first[:, :, i] = (part[i * 2, 1].astype(F32) + r_sib[i, 1].astype(F32)).astype(BF)
        return copy

    def y_sends(first, count):
        which = pl.ds(first, count)
        return [
            send(y_first.at[dy, other(yl, dl), which], r_y2.at[n, which], along_y[n])
            for n, (dy, dl) in enumerate(y_steps)
        ]

    wv_sib = weight_terms(0, lift_t, do_v)
    unit(2, 1)
    sib_2 = to_sib(2)
    unit(1, 1)
    sib_1 = to_sib(1)
    wv_plane = weight_sends(0, wv_sib)
    unit(2, 0)
    x_2 = on_chip(2, sib_2)
    unit(3, 1)
    sib_3 = to_sib(3)
    unit(1, 0)
    x_1 = on_chip(1, sib_1)
    unit(0, 1)
    sib_0 = to_sib(0)
    unit(3, 0)
    x_3 = on_chip(3, sib_3)
    y_late = y_sends(1, 3)
    unit(0, 0)
    on_chip(0, sib_0)
    y_last = y_sends(0, 1)

    def query_lift_grads():
        for c in range(4):
            rows = slice(c * 512, (c + 1) * 512)
            add = dot(four(c, WIDTH), ed[rows, :STACK])
            if c == 0:
                dql[...] = add
            else:
                dql[...] += add
        lift_t[...] = (dql[:LATENT, :] * SCALE).astype(BF)

    query_lift_grads()
    wk_sib = weight_terms(1, lift_t, q_nope)

    total = x_first[0].astype(F32)
    for n, copy in enumerate([x_1, x_2, x_3]):
        copy.wait_recv()
        total = total + r_x1[n].astype(F32)
    a_1[...] = total.astype(BF)
    y_sent = [
        send(a_1.at[dy, other(yl, dl)], r_y1.at[n], along_y[n])
        for n, (dy, dl) in enumerate(y_steps)
    ]
    total = y_first[0, yl].astype(F32)
    for n in range(3):
        y_late[n].wait_recv()
        y_last[n].wait_recv()
        total = total + r_y2[n].astype(F32)
    a_2[...] = total.astype(BF)
    x_sent = [send(a_2.at[i], r_x2.at[i - 1], along_x[i]) for i in range(1, 4)]
    wk_plane = weight_sends(1, wk_sib)

    def token_outputs():
        for h in range(HEADS_DEV):
            cols = slice(h * ROWS, (h + 1) * ROWS)
            dq_t[h * QK : h * QK + NOPE, :] = dot(wk_t[cols, :], lift_t[:, cols])
            dq_t[h * QK + NOPE : (h + 1) * QK, :] = dql[LATENT:, cols] * SCALE
        dq_ref[...] = dq_t[...].T.astype(BF)
        out_ref[...] = flip(o_t[...]).astype(BF)

    token_outputs()
    weight_end(0, wv_plane, dwv_ref)

    total = a_1[0, yl].astype(F32)
    for n, copy in enumerate(y_sent):
        copy.wait_recv()
        total = total + r_y1[n].astype(F32)
    to_z[:4] = total.reshape(4, 8, WIDTH)
    total = a_2[0].astype(F32)
    for n, copy in enumerate(x_sent):
        copy.wait_recv()
        total = total + r_x2[n].astype(F32)
    to_z[4:] = total.reshape(4, 8, WIDTH)
    z_sent = [
        send(to_z.at[lax.rem(z + d, 8)], r_z.at[d - 1], along_z[d - 1]) for d in range(1, 8)
    ]
    weight_end(1, wk_plane, dwk_ref)
    total = to_z[z]
    for d, copy in enumerate(z_sent):
        copy.wait_recv()
        total = total + r_z[d]
    dlat_ref[...] = total
    for copy in started:
        copy.wait_send()


COPIES = 64


def hand_on(*refs):
    sources, targets, sem = refs[:5], refs[5:10], refs[10]
    copies = [
        pltpu.make_async_copy(src, dst, sem.at[n])
        for n, (src, dst) in enumerate(zip(sources, targets))
    ]
    for copy in copies:
        copy.start()
    for copy in copies:
        copy.wait()


def on_device(latent, query, up_key, up_value, out_grad, block_pos):
    vmem = pltpu.VMEM
    scratch = [
        vmem((SEQ, WIDTH), BF),
        vmem((16, WIDTH, ROWS), BF),
        vmem((ROWS, HEADS_DEV * QK), BF),
        vmem((LATENT, STACK), BF),
        vmem((LATENT, STACK), BF),
        vmem((ROWS, STACK), BF),
        vmem((STACK, LATENT), BF),
        vmem((STACK, LATENT), BF),
        vmem((HEADS_DEV * QK, ROWS), BF),
        vmem((STACK, ROWS), BF),
        vmem((ROWS, STACK), BF),
        vmem((WIDTH, STACK), BF),
        vmem((2 * STACK, LATENT), BF),
        vmem((STACK, ROPE), BF),
        vmem((LATENT, STACK), F32),
        vmem((LATENT, STACK), BF),
        vmem((SEQ, STACK), F32),
        vmem((SEQ, 2 * STACK), BF),
        vmem((LATENT, STACK), F32),
        vmem((LATENT, STACK), BF),
        vmem((STACK, ROWS), BF),
        vmem((HEADS_DEV * QK, ROWS), F32),
        vmem((WIDTH, STACK), F32),
        vmem((8, STACK), F32),
        vmem((1, STACK), F32),
        vmem((8, 2, 2, 2, 32, WIDTH), BF),
        vmem((4, 2, 2, 2, 32, WIDTH), BF),
        vmem((4, 2, 2, 32, WIDTH), BF),
        vmem((3, 2, 2, 32, WIDTH), BF),
        vmem((2, 2, 32, WIDTH), BF),
        vmem((3, 32, WIDTH), BF),
        vmem((2, 2, 4, 32, WIDTH), BF),
        vmem((3, 4, 32, WIDTH), BF),
        vmem((4, 32, WIDTH), BF),
        vmem((3, 32, WIDTH), BF),
        vmem((8, 8, WIDTH), F32),
        vmem((7, 8, WIDTH), F32),
        vmem((2, 2, 8, 32, STACK), BF),
        vmem((2, 8, 32, STACK), BF),
        vmem((2, 8, 32, STACK), BF),
        vmem((2, 7, 32, STACK), BF),
        pltpu.SemaphoreType.DMA((5,)),
        pltpu.SemaphoreType.DMA((COPIES,)),
        pltpu.SemaphoreType.DMA((COPIES,)),
    ]
    hbm = pl.BlockSpec(memory_space=pl.ANY)
    in_vmem = pl.BlockSpec(memory_space=pltpu.VMEM)
    shapes = (
        jax.ShapeDtypeStruct((ROWS, STACK), BF),
        jax.ShapeDtypeStruct((ROWS, HEADS_DEV * QK), BF),
        jax.ShapeDtypeStruct((8, WIDTH), F32),
        jax.ShapeDtypeStruct((32, STACK), F32),
        jax.ShapeDtypeStruct((32, STACK), F32),
    )
    results = pl.pallas_call(
        kernel,
        out_shape=shapes,
        in_specs=[hbm] * 5 + [pl.BlockSpec(memory_space=pltpu.SMEM)],
        out_specs=[in_vmem] * 5,
        scratch_shapes=scratch,
        compiler_params=pltpu.CompilerParams(
            collective_id=0, has_side_effects=True, vmem_limit_bytes=56 * 1024 * 1024
        ),
        cost_estimate=pl.CostEstimate(
            flops=7_000_000_000, bytes_accessed=4_000_000, transcendentals=1_048_576
        ),
    )(latent.T, query, up_key, up_value, out_grad, block_pos)
    return tuple(
        pl.pallas_call(
            hand_on,
            out_shape=shapes,
            in_specs=[hbm] * 5,
            out_specs=[hbm] * 5,
            scratch_shapes=[pltpu.SemaphoreType.DMA((5,))],
            compiler_params=pltpu.CompilerParams(vmem_limit_bytes=60 * 1024 * 1024),
        )(*results)
    )


def solution(mesh):
    in_specs = (
        P("ctx", None),
        P("ctx", "head"),
        P(None, "head"),
        P(None, "head"),
        P("ctx", "head"),
        P(),
    )
    out_specs = (
        P("ctx", "head"),
        P("ctx", "head"),
        P(("ctx", "head"), None),
        P("ctx", "head"),
        P("ctx", "head"),
    )
    return jax.shard_map(
        on_device, mesh=mesh, in_specs=in_specs, out_specs=out_specs, check_vma=False
    )
```

```python
import functools
import math

import jax
import jax.numpy as jnp
from jax import lax
from jax.experimental import pallas as pl
from jax.experimental.pallas import tpu as pltpu
from jax.sharding import PartitionSpec as P

LATENT = 512
ROPE = 64
WIDTH = LATENT + ROPE
NOPE = 128
VDIM = 128
QK = NOPE + ROPE
ROWS = 128
HEADS_DEV = 4
STACK = HEADS_DEV * ROWS
SEQ = 2048
SCALE = 1.0 / math.sqrt(QK)
LOG2E = 1.4426950408889634
MASKED = -1e30

BF = jnp.bfloat16
F32 = jnp.float32


def dot(a, b):
    return jnp.dot(a, b, preferred_element_type=F32)


def flip(a):
    return a.astype(F32).T


def slot(i, dk, dy):
    return i * 4 + dk * 2 + dy


def other(a, flip_it):
    return 1 - a if flip_it else a


def kernel(
    latent_t_hbm, query_hbm, wk_hbm, wv_hbm, dout_hbm, bpos,
    out_ref, dq_ref, dlat_ref, dwk_ref, dwv_ref,
    lat, lat_t, q_v, wk, wv, do_v, wk_t, wv_t, q_t, do_t, q_nope,
    qs_t, qd, q_rope, dlift, dos_t, scores, ed, lift_acc, lift_t, o_t, dq_t, dql,
    top, delta_row, part, r_sib, x_first, r_x1, a_1, r_y1, y_first, r_y2, a_2, r_x2,
    to_z, r_z, w_own, w_sib, w_acc, w_r,
    out_v, dq_v, dlat_v, dwk_v, dwv_v, load_sem, store_sem, send_sem, recv_sem,
):
    ctx, head = lax.axis_index("ctx"), lax.axis_index("head")
    x, yh, core = lax.div(ctx, 4), lax.rem(lax.div(ctx, 2), 2), lax.rem(ctx, 2)
    z, yl = lax.div(head, 2), lax.rem(head, 2)

    def x_at(i):
        return lax.rem(x + i, 4)

    def dev(i, dy, dk, dz, dl):
        xx, yy, kk = x_at(i), other(yh, dy), other(core, dk)
        return ((xx * 2 + yy) * 2 + kk, lax.rem(z + dz, 8) * 2 + other(yl, dl))

    sib = dev(0, 0, 1, 0, 0)
    near_y = dev(0, 1, 0, 0, 1)
    along_x = [None] + [dev(i, 0, 0, 0, 0) for i in range(1, 4)]
    y_steps = [(0, 1), (1, 0), (1, 1)]
    along_y = [dev(0, dy, 0, 0, dl) for dy, dl in y_steps]
    along_z = [dev(0, 0, 0, d, 0) for d in range(1, 8)]

    plane_steps = [(i, dy) for i in range(4) for dy in range(2)][1:]
    plane = [dev(i, dy, 0, 0, 0) for i, dy in plane_steps]

    loads = [
        pltpu.make_async_copy(src, dst, load_sem.at[n])
        for n, (src, dst) in enumerate(
            [
                (latent_t_hbm, lat_t.at[0]),
                (query_hbm, q_v),
                (wk_hbm, wk),
                (dout_hbm, do_v),
                (wv_hbm, wv),
            ]
        )
    ]
    for load in loads:
        load.start()

    barrier = pltpu.get_barrier_semaphore()
    partners = [sib] + plane + [along_y[0], along_y[2]] + along_z
    for partner in partners:
        pl.semaphore_signal(barrier, inc=1, device_id=partner, device_id_type=pl.DeviceIdType.MESH)
    pl.semaphore_wait(barrier, len(partners))

    started = []

    def send(src, dst, to):
        n = len(started)
        assert n < COPIES
        copy = pltpu.make_async_remote_copy(
            src_ref=src, dst_ref=dst, send_sem=send_sem.at[n], recv_sem=recv_sem.at[n],
            device_id=to, device_id_type=pl.DeviceIdType.MESH,
        )
        copy.start()
        started.append(copy)
        return copy

    def block(i, dk, dy, h=None):
        if h is None:
            return lat_t.at[slot(i, dk, dy)]
        return lat_t.at[slot(i, dk, dy), pl.ds(h * (WIDTH // 2), WIDTH // 2)]

    def send_halves(src, dst, to):
        return [send(block(*src, h), block(*dst, h), to) for h in range(2)]

    def pass_on(i, dy):
        return send(block(i, 0, dy), block(i, 1, dy), sib)

    loads[0].wait()
    from_x2 = send_halves((0, 0, 0), (2, 0, 0), along_x[2])
    from_y = send_halves((0, 0, 0), (0, 0, 1), near_y)
    sib_got = {(0, 0): pass_on(0, 0)}

    for load in loads[1:]:
        load.wait()

    def lift_queries():
        q_t[...] = flip(q_v[...]).astype(BF)
        for h in range(HEADS_DEV):
            cols = slice(h * ROWS, (h + 1) * ROWS)
            q_h_t = q_t[h * QK : h * QK + NOPE, :]
            q_lift = dot(wk[:, cols], q_h_t)
            qs_t[:LATENT, cols] = (q_lift * (SCALE * LOG2E)).astype(BF)
            rope_t = q_t[h * QK + NOPE : (h + 1) * QK, :].astype(F32)
            qs_t[LATENT:, cols] = (rope_t * (SCALE * LOG2E)).astype(BF)

    from_x3 = send(block(0, 0, 0), block(3, 0, 0), along_x[1])
    from_x1 = send(block(0, 0, 0), block(1, 0, 0), along_x[3])
    lift_queries()
    query_row = lax.broadcasted_iota(jnp.int32, (1, STACK), 1)
    query_pos = (
        jnp.where(lax.rem(query_row, 128) < 64, bpos[2 * ctx], bpos[2 * ctx + 1]) * 64
        + lax.rem(query_row, 64)
    )
    top[...] = jnp.full(top.shape, MASKED, F32)
    key_row = lax.broadcasted_iota(jnp.int32, (ROWS, 1), 0)

    def score_block(i, dk, dy):
        rows = pl.ds(slot(i, dk, dy) * ROWS, ROWS)
        owner = (x_at(i) * 2 + other(yh, dy)) * 2 + other(core, dk)
        keys = flip(lat_t[slot(i, dk, dy)]).astype(BF)
        lat[rows, :] = keys
        key_pos = (
            jnp.where(key_row < 64, bpos[2 * owner], bpos[2 * owner + 1]) * 64
            + lax.rem(key_row, 64)
        )
        s = jnp.where(key_pos <= query_pos, dot(keys, qs_t[...]), MASKED)
        scores[rows, :] = s
        top[...] = jnp.maximum(top[...], jnp.max(s.reshape(ROWS // 8, 8, STACK), axis=0))

    score_block(0, 0, 0)
    up_x3, up_x1, up_y = [], [], []
    for h in range(2):
        from_y[h].wait_recv()
        up_x3.append(send(block(0, 0, 1, h), block(3, 0, 1, h), along_x[1]))
        up_x1.append(send(block(0, 0, 1, h), block(1, 0, 1, h), along_x[3]))
    sib_got[0, 1] = pass_on(0, 1)
    sib_got[0, 0].wait_recv()
    score_block(0, 1, 0)
    for h in range(2):
        from_x2[h].wait_recv()
        up_y.append(send(block(2, 0, 0, h), block(2, 0, 1, h), near_y))
    sib_got[2, 0] = pass_on(2, 0)
    score_block(0, 0, 1)
    from_x3.wait_recv()
    sib_got[3, 0] = pass_on(3, 0)
    from_x1.wait_recv()
    sib_got[1, 0] = pass_on(1, 0)
    score_block(2, 0, 0)
    score_block(3, 0, 0)
    score_block(1, 0, 0)

    def lift_rest():
        wk_t[...] = flip(wk[...]).astype(BF)
        wv_t[...] = flip(wv[...]).astype(BF)
        do_t[...] = flip(do_v[...]).astype(BF)
        for h in range(HEADS_DEV):
            cols = slice(h * ROWS, (h + 1) * ROWS)
            q_nope[:, cols] = flip(q_t[h * QK : h * QK + NOPE, :]).astype(BF)
            rope = flip(q_t[h * QK + NOPE : (h + 1) * QK, :])
            q_rope[cols, :] = (rope * SCALE).astype(BF)
            qd[cols, :] = (dot(q_nope[:, cols], wk_t[cols, :]) * SCALE).astype(BF)
            dlift[:, cols] = dot(wv[:, cols], do_t[cols, :])

    lift_rest()
    sib_got[0, 1].wait_recv()
    score_block(0, 1, 1)
    sib_got[2, 0].wait_recv()
    score_block(2, 1, 0)
    for h in range(2):
        up_x3[h].wait_recv()
    sib_got[3, 1] = pass_on(3, 1)
    for h in range(2):
        up_x1[h].wait_recv()
    sib_got[1, 1] = pass_on(1, 1)
    sib_got[3, 0].wait_recv()
    score_block(3, 1, 0)
    sib_got[1, 0].wait_recv()
    score_block(1, 1, 0)
    for h in range(2):
        up_y[h].wait_recv()
    sib_got[2, 1] = pass_on(2, 1)
    score_block(3, 0, 1)
    score_block(1, 0, 1)
    score_block(2, 0, 1)
    sib_got[3, 1].wait_recv()
    score_block(3, 1, 1)
    sib_got[1, 1].wait_recv()
    score_block(1, 1, 1)
    sib_got[2, 1].wait_recv()
    score_block(2, 1, 1)

    def four(c, width):
        return jnp.concatenate([lat_t[c * 4 + n, :width, :] for n in range(4)], axis=1)

    def forward():
        row_max = jnp.max(top[...], axis=0, keepdims=True)
        total = jnp.zeros((8, STACK), F32)
        for c in range(4):
            rows = slice(c * 512, (c + 1) * 512)
            e = jnp.exp2(scores[rows, :] - row_max)
            total = total + jnp.sum(e.reshape(64, 8, STACK), axis=0)
            ed[rows, STACK:] = e.astype(BF)
            add = dot(four(c, LATENT), ed[rows, STACK:])
            if c == 0:
                lift_acc[...] = add
            else:
                lift_acc[...] += add
        inverse = 1.0 / jnp.sum(total, axis=0, keepdims=True)
        lift_t[...] = (lift_acc[...] * inverse).astype(BF)
        deltas = []
        for h in range(HEADS_DEV):
            cols = slice(h * ROWS, (h + 1) * ROWS)
            o_low = dot(wv_t[cols, :], lift_t[:, cols]).astype(BF)
            o_t[cols, :] = o_low
            deltas.append(
                jnp.sum(do_t[cols, :].astype(F32) * o_low.astype(F32), axis=0, keepdims=True)
            )
            scaled = dlift[:, cols] * inverse[:, cols]
            dos_t[:, cols] = scaled.astype(BF)
            qd[STACK + h * ROWS : STACK + (h + 1) * ROWS, :] = scaled.T.astype(BF)
        delta_row[...] = jnp.concatenate(deltas, axis=1) * inverse

    forward()

    def weight_terms(n, lifted, by):
        for h in range(HEADS_DEV):
            cols = slice(h * ROWS, (h + 1) * ROWS)
            g = dot(lifted[:, cols], by[:, cols]).astype(BF)
            for piece in range(16):
                xx, yy, kk = piece // 4, piece // 2 % 2, piece % 2
                w_own[n, kk, yy, xx, :, cols] = g[piece * 32 : (piece + 1) * 32, :]
        return send(w_own.at[n, 1 - core], w_sib.at[n], sib)

    def weight_on_chip(n, arrived):
        arrived.wait_recv()
        w_acc[n] = (w_own[n, core].astype(F32) + w_sib[n].astype(F32)).astype(BF)

    def weight_sends(n):
        return [
            send(w_acc.at[n, other(yh, dy), x_at(i)], w_r.at[n, m], plane[m])
            for m, (i, dy) in enumerate(plane_steps)
        ]

    def summed(total, ref, arrived):
        for n, copy in enumerate(arrived):
            copy.wait_recv()
            total = total + ref[n].astype(F32)
        return total

    def unit(i, dk):
        u = i * 2 + dk
        rows = slice(u * 256, (u + 1) * 256)
        dp = dot(lat[rows, :LATENT], dos_t[...])
        ds = (ed[rows, STACK:].astype(F32) * (dp - delta_row[...])).astype(BF)
        ed[rows, :STACK] = ds
        nope = dot(ed[rows, :], qd[...])
        rope = dot(ds, q_rope[...])
        for half in range(2):
            for dy in range(2):
                for low in range(2):
                    starts = [dy * 128 + half * 64 + n * 16 + low * 8 for n in range(4)]
                    part[u, half, dy, low, :, :LATENT] = jnp.concatenate(
                        [nope[r : r + 8, :] for r in starts], axis=0
                    ).astype(BF)
                    part[u, half, dy, low, :, LATENT:] = jnp.concatenate(
                        [rope[r : r + 8, :] for r in starts], axis=0
                    ).astype(BF)

    def y_sends(i):
        return [
            send(y_first.at[dy, other(yl, dl), i], r_y2.at[n, i], along_y[n])
            for n, (dy, dl) in enumerate(y_steps)
        ]

    def to_sib(i):
        return send(part.at[i * 2 + 1], r_sib.at[i], sib)

    def on_chip(i, arrived):
        arrived.wait_recv()
        x_first[i] = (part[i * 2, 0].astype(F32) + r_sib[i, 0].astype(F32)).astype(BF)
        copy = send(x_first.at[i], r_x1.at[i - 1], along_x[i]) if i else None
        y_first[:, :, i] = (part[i * 2, 1].astype(F32) + r_sib[i, 1].astype(F32)).astype(BF)
        return copy, y_sends(i)

    def x_after_y(i, copies):
        a_2[i] = summed(y_first[0, yl, i].astype(F32), r_y2.at[:, i], copies).astype(BF)
        return send(a_2.at[i], r_x2.at[i - 1], along_x[i]) if i else None

    unit(2, 1)
    sib_2 = to_sib(2)
    unit(2, 0)
    wv_sib = weight_terms(0, lift_t, do_v)
    unit(1, 1)
    sib_1 = to_sib(1)
    x_2, y_2 = on_chip(2, sib_2)
    unit(1, 0)
    unit(3, 1)
    sib_3 = to_sib(3)
    x_1, y_1 = on_chip(1, sib_1)
    unit(3, 0)
    unit(0, 1)
    sib_0 = to_sib(0)
    x_3, y_3 = on_chip(3, sib_3)
    unit(0, 0)
    _, y_0 = on_chip(0, sib_0)
    weight_on_chip(0, wv_sib)
    x_sent = [x_after_y(2, y_2)]
    wv_got = weight_sends(0)

    def query_lift_grads():
        for c in range(4):
            rows = slice(c * 512, (c + 1) * 512)
            add = dot(four(c, WIDTH), ed[rows, :STACK])
            if c == 0:
                dql[...] = add
            else:
                dql[...] += add
        lift_t[...] = (dql[:LATENT, :] * SCALE).astype(BF)

    query_lift_grads()
    wk_sib = weight_terms(1, lift_t, q_nope)

    def token_outputs():
        for h in range(HEADS_DEV):
            cols = slice(h * ROWS, (h + 1) * ROWS)
            dq_t[h * QK : h * QK + NOPE, :] = dot(wk_t[cols, :], lift_t[:, cols])
            dq_t[h * QK + NOPE : (h + 1) * QK, :] = dql[LATENT:, cols] * SCALE
        dq_v[...] = dq_t[...].T.astype(BF)
        out_v[...] = flip(o_t[...]).astype(BF)

    token_outputs()
    stored = []

    def store(src, dst):
        copy = pltpu.make_async_copy(src, dst, store_sem.at[len(stored)])
        copy.start()
        stored.append(copy)

    store(dq_v, dq_ref)
    store(out_v, out_ref)

    x_sent.insert(0, x_after_y(1, y_1))
    a_1[...] = summed(x_first[0].astype(F32), r_x1, [x_1, x_2, x_3]).astype(BF)
    y_sent = [
        send(a_1.at[dy, other(yl, dl)], r_y1.at[n], along_y[n])
        for n, (dy, dl) in enumerate(y_steps)
    ]
    x_sent.append(x_after_y(3, y_3))
    x_after_y(0, y_0)
    weight_on_chip(1, wk_sib)
    wk_got = weight_sends(1)

    to_z[:4] = summed(a_1[0, yl].astype(F32), r_y1, y_sent).reshape(4, 8, WIDTH)
    to_z[4:] = summed(a_2[0].astype(F32), r_x2, x_sent).reshape(4, 8, WIDTH)
    z_sent = [
        send(to_z.at[lax.rem(z + d, 8)], r_z.at[d - 1], along_z[d - 1]) for d in range(1, 8)
    ]
    dwv_v[...] = summed(w_acc[0, yh, x].astype(F32), w_r.at[0], wv_got)
    store(dwv_v, dwv_ref)
    dwk_v[...] = summed(w_acc[1, yh, x].astype(F32), w_r.at[1], wk_got)
    store(dwk_v, dwk_ref)
    dlat_v[...] = summed(to_z[z], r_z, z_sent)
    store(dlat_v, dlat_ref)
    for copy in stored:
        copy.wait()
    for copy in started:
        copy.wait_send()


COPIES = 72


def hand_on(*refs):
    sources, targets, held, sem = refs[:5], refs[5:10], refs[10:15], refs[15]
    arriving = [pltpu.make_async_copy(a, b, sem.at[0, n]) for n, (a, b) in enumerate(zip(sources, held))]
    leaving = [pltpu.make_async_copy(a, b, sem.at[1, n]) for n, (a, b) in enumerate(zip(held, targets))]
    for copy in arriving:
        copy.start()
    for before, after in zip(arriving, leaving):
        before.wait()
        after.start()
    for copy in leaving:
        copy.wait()


def on_device(latent, query, up_key, up_value, out_grad, block_pos):
    vmem = pltpu.VMEM
    shapes = (
        jax.ShapeDtypeStruct((ROWS, STACK), BF),
        jax.ShapeDtypeStruct((ROWS, HEADS_DEV * QK), BF),
        jax.ShapeDtypeStruct((8, WIDTH), F32),
        jax.ShapeDtypeStruct((32, STACK), F32),
        jax.ShapeDtypeStruct((32, STACK), F32),
    )
    scratch = [
        vmem((SEQ, WIDTH), BF),
        vmem((16, WIDTH, ROWS), BF),
        vmem((ROWS, HEADS_DEV * QK), BF),
        vmem((LATENT, STACK), BF),
        vmem((LATENT, STACK), BF),
        vmem((ROWS, STACK), BF),
        vmem((STACK, LATENT), BF),
        vmem((STACK, LATENT), BF),
        vmem((HEADS_DEV * QK, ROWS), BF),
        vmem((STACK, ROWS), BF),
        vmem((ROWS, STACK), BF),
        vmem((WIDTH, STACK), BF),
        vmem((2 * STACK, LATENT), BF),
        vmem((STACK, ROPE), BF),
        vmem((LATENT, STACK), F32),
        vmem((LATENT, STACK), BF),
        vmem((SEQ, STACK), F32),
        vmem((SEQ, 2 * STACK), BF),
        vmem((LATENT, STACK), F32),
        vmem((LATENT, STACK), BF),
        vmem((STACK, ROWS), BF),
        vmem((HEADS_DEV * QK, ROWS), F32),
        vmem((WIDTH, STACK), F32),
        vmem((8, STACK), F32),
        vmem((1, STACK), F32),
        vmem((8, 2, 2, 2, 32, WIDTH), BF),
        vmem((4, 2, 2, 2, 32, WIDTH), BF),
        vmem((4, 2, 2, 32, WIDTH), BF),
        vmem((3, 2, 2, 32, WIDTH), BF),
        vmem((2, 2, 32, WIDTH), BF),
        vmem((3, 32, WIDTH), BF),
        vmem((2, 2, 4, 32, WIDTH), BF),
        vmem((3, 4, 32, WIDTH), BF),
        vmem((4, 32, WIDTH), BF),
        vmem((3, 32, WIDTH), BF),
        vmem((8, 8, WIDTH), F32),
        vmem((7, 8, WIDTH), F32),
        vmem((2, 2, 2, 4, 32, STACK), BF),
        vmem((2, 2, 4, 32, STACK), BF),
        vmem((2, 2, 4, 32, STACK), BF),
        vmem((2, 7, 32, STACK), BF),
    ]
    scratch += [vmem(shape.shape, shape.dtype) for shape in shapes]
    scratch += [
        pltpu.SemaphoreType.DMA((5,)),
        pltpu.SemaphoreType.DMA((5,)),
        pltpu.SemaphoreType.DMA((COPIES,)),
        pltpu.SemaphoreType.DMA((COPIES,)),
    ]
    hbm = pl.BlockSpec(memory_space=pl.ANY)
    results = pl.pallas_call(
        kernel,
        out_shape=shapes,
        in_specs=[hbm] * 5 + [pl.BlockSpec(memory_space=pltpu.SMEM)],
        out_specs=[hbm] * 5,
        scratch_shapes=scratch,
        compiler_params=pltpu.CompilerParams(
            collective_id=0, has_side_effects=True, vmem_limit_bytes=56 * 1024 * 1024
        ),
        cost_estimate=pl.CostEstimate(
            flops=7_000_000_000, bytes_accessed=4_000_000, transcendentals=1_048_576
        ),
    )(latent.T, query, up_key, up_value, out_grad, block_pos)
    return tuple(
        pl.pallas_call(
            hand_on,
            out_shape=shapes,
            in_specs=[hbm] * 5,
            out_specs=[hbm] * 5,
            scratch_shapes=[vmem(shape.shape, shape.dtype) for shape in shapes]
            + [pltpu.SemaphoreType.DMA((2, 5))],
            compiler_params=pltpu.CompilerParams(vmem_limit_bytes=60 * 1024 * 1024),
        )(*results)
    )


def solution(mesh):
    in_specs = (
        P("ctx", None),
        P("ctx", "head"),
        P(None, "head"),
        P(None, "head"),
        P("ctx", "head"),
        P(),
    )
    out_specs = (
        P("ctx", "head"),
        P("ctx", "head"),
        P(("ctx", "head"), None),
        P("ctx", "head"),
        P("ctx", "head"),
    )
    return jax.shard_map(
        on_device, mesh=mesh, in_specs=in_specs, out_specs=out_specs, check_vma=False
    )
```

```python
import functools
import math

import jax
import jax.numpy as jnp
from jax import lax
from jax.experimental import pallas as pl
from jax.experimental.pallas import tpu as pltpu
from jax.sharding import PartitionSpec as P

LATENT = 512
ROPE = 64
WIDTH = LATENT + ROPE
NOPE = 128
VDIM = 128
QK = NOPE + ROPE
ROWS = 128
HEADS_DEV = 4
STACK = HEADS_DEV * ROWS
SEQ = 2048
HALF = WIDTH // 2
SCALE = 1.0 / math.sqrt(QK)
LOG2E = 1.4426950408889634
MASKED = -1e30

BF = jnp.bfloat16
F32 = jnp.float32


def dot(a, b):
    return jnp.dot(a, b, preferred_element_type=F32)


def flip(a):
    return a.astype(F32).T


EARLY = 10


def slot(i, dk, dy):
    if i and dy:
        return EARLY + (i - 1) * 2 + dk
    return (dy if i == 0 else i + 1) * 2 + dk


def other(a, flip_it):
    return 1 - a if flip_it else a


def kernel(
    latent_t_hbm, query_hbm, wk_hbm, wv_hbm, dout_hbm, bpos,
    out_ref, dq_ref, dlat_ref, dwk_ref, dwv_ref,
    lat, lat_t, q_v, wk, wv, do_v, wk_t, wv_t, q_t, do_t, q_nope,
    qs_t, qd, q_rope, dlift, dos_t, scores, ed, lift_acc, lift_t, o_t, dq_t, dql,
    top, stats, rescale_row, inverse_row, delta_row, part, r_sib, x_first, r_x1, r_pair, x_half, r_half, a_1, r_y1, y_first, r_y2, a_2, r_x2,
    to_z, r_z, w_own, w_sib, w_acc, w_x, w_col, w_y,
    load_sem, ring_sem, send_sem, recv_sem,
):
    ctx, head = lax.axis_index("ctx"), lax.axis_index("head")
    x, yh, core = lax.div(ctx, 4), lax.rem(lax.div(ctx, 2), 2), lax.rem(ctx, 2)
    z, yl = lax.div(head, 2), lax.rem(head, 2)

    def x_at(i):
        return lax.rem(x + i, 4)

    def dev(i, dy, dk, dz, dl):
        xx, yy, kk = x_at(i), other(yh, dy), other(core, dk)
        return ((xx * 2 + yy) * 2 + kk, lax.rem(z + dz, 8) * 2 + other(yl, dl))

    sib = dev(0, 0, 1, 0, 0)
    near_y = dev(0, 1, 0, 0, 1)
    along_x = [None] + [dev(i, 0, 0, 0, 0) for i in range(1, 4)]
    y_steps = [(0, 1), (1, 0), (1, 1)]
    along_y = [dev(0, dy, 0, 0, dl) for dy, dl in y_steps]
    along_z = [dev(0, 0, 0, d, 0) for d in range(1, 8)]

    parity = lax.rem(z, 2)

    loads = [
        pltpu.make_async_copy(src, dst, load_sem.at[n])
        for n, (src, dst) in enumerate(
            [
                (latent_t_hbm, lat_t.at[0]),
                (query_hbm, q_v),
                (wk_hbm, wk),
                (dout_hbm, do_v),
                (wv_hbm, wv),
            ]
        )
    ]
    for load in loads:
        load.start()

    barrier = pltpu.get_barrier_semaphore()
    partners = [sib] + along_x[1:] + along_y + [along_z[0], along_z[6]]
    for partner in partners:
        pl.semaphore_signal(barrier, inc=1, device_id=partner, device_id_type=pl.DeviceIdType.MESH)
    pl.semaphore_wait(barrier, len(partners))

    def greet(n, d):
        for to in (along_z[d - 1], along_z[7 - d]):
            pl.semaphore_signal(
                ring_sem.at[n], inc=1, device_id=to, device_id_type=pl.DeviceIdType.MESH
            )

    greet(0, 1)

    started = []

    def send(src, dst, to):
        n = len(started)
        assert n < COPIES
        copy = pltpu.make_async_remote_copy(
            src_ref=src, dst_ref=dst, send_sem=send_sem.at[n], recv_sem=recv_sem.at[n],
            device_id=to, device_id_type=pl.DeviceIdType.MESH,
        )
        copy.start()
        started.append(copy)
        return copy

    def block(i, dk, dy, h=None):
        if h is None:
            return lat_t.at[slot(i, dk, dy)]
        return lat_t.at[slot(i, dk, dy), pl.ds(pl.multiple_of(h * HALF, 16), HALF)]

    def send_halves(src, dst, to):
        return [send(block(*src, h), block(*dst, h), to) for h in range(2)]

    def trade_quarters(*where):
        copies = []
        for q, to in ((0, along_z[0]), (1, along_z[6])):
            rows = pl.ds(pl.multiple_of(parity * HALF + q * (HALF // 2), 16), HALF // 2)
            quarter = lat_t.at[slot(*where), rows]
            copies.append(send(quarter, quarter, to))
        return copies

    def pass_on(i, dy):
        return send(block(i, 0, dy), block(i, 1, dy), sib)

    loads[0].wait()
    from_x2 = send(block(0, 0, 0, parity), block(2, 0, 0, parity), along_x[2])
    from_y = send_halves((0, 0, 0), (0, 0, 1), near_y)
    sib_got = {(0, 0): pass_on(0, 0)}

    for load in loads[1:]:
        load.wait()

    def lift_queries():
        q_t[...] = flip(q_v[...]).astype(BF)
        for h in range(HEADS_DEV):
            cols = slice(h * ROWS, (h + 1) * ROWS)
            q_h_t = q_t[h * QK : h * QK + NOPE, :]
            q_lift = dot(wk[:, cols], q_h_t)
            qs_t[:LATENT, cols] = (q_lift * (SCALE * LOG2E)).astype(BF)
            rope_t = q_t[h * QK + NOPE : (h + 1) * QK, :].astype(F32)
            qs_t[LATENT:, cols] = (rope_t * (SCALE * LOG2E)).astype(BF)

    from_x3 = send(block(0, 0, 0), block(3, 0, 0), along_x[1])
    from_x1 = send(block(0, 0, 0), block(1, 0, 0), along_x[3])
    lift_queries()
    query_row = lax.broadcasted_iota(jnp.int32, (1, STACK), 1)
    query_pos = (
        jnp.where(lax.rem(query_row, 128) < 64, bpos[2 * ctx], bpos[2 * ctx + 1]) * 64
        + lax.rem(query_row, 64)
    )
    top[...] = jnp.full(top.shape, MASKED, F32)
    key_row = lax.broadcasted_iota(jnp.int32, (ROWS, 1), 0)

    def score_block(i, dk, dy):
        rows = pl.ds(slot(i, dk, dy) * ROWS, ROWS)
        owner = (x_at(i) * 2 + other(yh, dy)) * 2 + other(core, dk)
        keys = flip(lat_t[slot(i, dk, dy)]).astype(BF)
        lat[rows, :] = keys
        key_pos = (
            jnp.where(key_row < 64, bpos[2 * owner], bpos[2 * owner + 1]) * 64
            + lax.rem(key_row, 64)
        )
        s = jnp.where(key_pos <= query_pos, dot(keys, qs_t[...]), MASKED)
        scores[rows, :] = s
        top[...] = jnp.maximum(top[...], jnp.max(s.reshape(ROWS // 8, 8, STACK), axis=0))

    score_block(0, 0, 0)
    pl.semaphore_wait(ring_sem.at[0], 2)
    greet(1, 2)
    up_x3, up_x1 = [], []

    def up_x(h):
        from_y[h].wait_recv()
        up_x3.append(send(block(0, 0, 1, h), block(3, 0, 1, h), along_x[1]))
        up_x1.append(send(block(0, 0, 1, h), block(1, 0, 1, h), along_x[3]))

    up_x(0)
    from_x2.wait_recv()
    up_y = [send(block(2, 0, 0, parity), block(2, 0, 1, parity), near_y)]
    traded = trade_quarters(2, 0, 0)
    up_x(1)
    sib_got[0, 1] = pass_on(0, 1)
    sib_got[0, 0].wait_recv()
    score_block(0, 1, 0)
    from_x3.wait_recv()
    sib_got[3, 0] = pass_on(3, 0)
    from_x1.wait_recv()
    sib_got[1, 0] = pass_on(1, 0)
    score_block(0, 0, 1)
    for copy in traded:
        copy.wait_recv()
    up_y.append(send(block(2, 0, 0, 1 - parity), block(2, 0, 1, 1 - parity), near_y))
    sib_got[2, 0] = pass_on(2, 0)
    score_block(3, 0, 0)
    score_block(1, 0, 0)

    def lift_rest():
        wk_t[...] = flip(wk[...]).astype(BF)
        wv_t[...] = flip(wv[...]).astype(BF)
        do_t[...] = flip(do_v[...]).astype(BF)
        for h in range(HEADS_DEV):
            cols = slice(h * ROWS, (h + 1) * ROWS)
            q_nope[:, cols] = flip(q_t[h * QK : h * QK + NOPE, :]).astype(BF)
            rope = flip(q_t[h * QK + NOPE : (h + 1) * QK, :])
            q_rope[cols, :] = (rope * SCALE).astype(BF)
            qd[cols, :] = (dot(q_nope[:, cols], wk_t[cols, :]) * SCALE).astype(BF)
            dlift[:, cols] = dot(wv[:, cols], do_t[cols, :])

    lift_rest()
    pl.semaphore_wait(ring_sem.at[1], 2)
    sib_got[0, 1].wait_recv()
    score_block(0, 1, 1)
    score_block(2, 0, 0)
    sib_got[3, 0].wait_recv()
    score_block(3, 1, 0)
    sib_got[1, 0].wait_recv()
    score_block(1, 1, 0)
    sib_got[2, 0].wait_recv()
    score_block(2, 1, 0)

    def side_by_side(first, count, width):
        return jnp.concatenate(
            [lat_t[first + n, :width, :] for n in range(count)], axis=1
        )

    def exponentials(first, last, row_max):
        total = jnp.zeros((8, STACK), F32)
        for start in range(first, last, 4):
            count = min(4, last - start)
            rows = slice(start * ROWS, (start + count) * ROWS)
            e = jnp.exp2(scores[rows, :] - row_max)
            total = total + jnp.sum(e.reshape(count * ROWS // 8, 8, STACK), axis=0)
            ed[rows, STACK:] = e.astype(BF)
            add = dot(side_by_side(start, count, LATENT), ed[rows, STACK:])
            if start == 0:
                lift_acc[...] = add
            else:
                lift_acc[...] += add
        return jnp.sum(total, axis=0, keepdims=True)

    def forward_early():
        early_max = jnp.max(top[...], axis=0, keepdims=True)
        stats[0:1, :] = early_max
        stats[1:2, :] = exponentials(0, EARLY, early_max)

    def forward_sum():
        early_max = stats[0:1, :]
        row_max = jnp.max(top[...], axis=0, keepdims=True)
        rescale = jnp.exp2(early_max - row_max)
        rescale_row[...] = rescale
        lift_acc[...] = lift_acc[...] * rescale
        total = stats[1:2, :] * rescale + exponentials(EARLY, 16, row_max)
        inverse = 1.0 / total
        lift_t[...] = (lift_acc[...] * inverse).astype(BF)
        inverse_row[...] = inverse

    def forward_rest():
        inverse = inverse_row[...]
        deltas = []
        for h in range(HEADS_DEV):
            cols = slice(h * ROWS, (h + 1) * ROWS)
            o_low = dot(wv_t[cols, :], lift_t[:, cols]).astype(BF)
            o_t[cols, :] = o_low
            deltas.append(
                jnp.sum(do_t[cols, :].astype(F32) * o_low.astype(F32), axis=0, keepdims=True)
            )
            scaled = dlift[:, cols] * inverse[:, cols]
            dos_t[:, cols] = scaled.astype(BF)
            qd[STACK + h * ROWS : STACK + (h + 1) * ROWS, :] = scaled.T.astype(BF)
        delta_row[...] = jnp.concatenate(deltas, axis=1) * inverse

    forward_early()
    for h in range(2):
        up_x3[h].wait_recv()
    sib_got[3, 1] = pass_on(3, 1)
    for h in range(2):
        up_x1[h].wait_recv()
    sib_got[1, 1] = pass_on(1, 1)
    for copy in up_y:
        copy.wait_recv()
    sib_got[2, 1] = pass_on(2, 1)
    score_block(3, 0, 1)
    score_block(1, 0, 1)
    score_block(2, 0, 1)
    sib_got[3, 1].wait_recv()
    score_block(3, 1, 1)
    sib_got[1, 1].wait_recv()
    score_block(1, 1, 1)
    sib_got[2, 1].wait_recv()
    score_block(2, 1, 1)

    def weight_terms(n, lifted, by):
        for h in range(HEADS_DEV):
            cols = slice(h * ROWS, (h + 1) * ROWS)
            g = dot(lifted[:, cols], by[:, cols]).astype(BF)
            for piece in range(16):
                xx, yy, kk = piece // 4, piece // 2 % 2, piece % 2
                w_own[n, kk, yy, xx, :, cols] = g[piece * 32 : (piece + 1) * 32, :]
        return send(w_own.at[n, 1 - core], w_sib.at[n], sib)

    def weight_on_chip(n, arrived):
        arrived.wait_recv()
        w_acc[n] = (w_own[n, core].astype(F32) + w_sib[n].astype(F32)).astype(BF)
        return [
            send(w_acc.at[n, :, x_at(i)], w_x.at[n, i - 1], along_x[i]) for i in range(1, 4)
        ]

    def weight_on_y(n, arrived):
        w_col[n] = summed(w_acc[n, :, x].astype(F32), w_x.at[n], arrived).astype(BF)
        return send(w_col.at[n, 1 - yh], w_y.at[n], along_y[1])

    def weight_end(n, arrived):
        arrived.wait_recv()
        return w_col[n, yh].astype(F32) + w_y[n].astype(F32)

    def summed(total, ref, arrived):
        for n, copy in enumerate(arrived):
            copy.wait_recv()
            total = total + ref[n].astype(F32)
        return total

    def unit(i, dk):
        u = i * 2 + dk
        spans = [pl.ds(slot(i, dk, dy) * ROWS, ROWS) for dy in range(2)]

        def both(ref, cols):
            return jnp.concatenate([ref[rows, cols] for rows in spans], axis=0)

        dp = dot(both(lat, slice(0, LATENT)), dos_t[...])
        for dy, rows in enumerate(spans):
            e = ed[rows, STACK:].astype(F32)
            if slot(i, dk, dy) < EARLY:
                e = e * rescale_row[...]
                ed[rows, STACK:] = e.astype(BF)
            ds = e * (dp[dy * ROWS : (dy + 1) * ROWS] - delta_row[...])
            ed[rows, :STACK] = ds.astype(BF)
        nope = dot(both(ed, slice(None)), qd[...])
        rope = dot(both(ed, slice(0, STACK)), q_rope[...])
        for half in range(2):
            for dy in range(2):
                for low in range(2):
                    starts = [dy * 128 + half * 64 + n * 16 + low * 8 for n in range(4)]
                    part[u, half, dy, low, :, :LATENT] = jnp.concatenate(
                        [nope[r : r + 8, :] for r in starts], axis=0
                    ).astype(BF)
                    part[u, half, dy, low, :, LATENT:] = jnp.concatenate(
                        [rope[r : r + 8, :] for r in starts], axis=0
                    ).astype(BF)

    def y_sends(i):
        return [
            send(y_first.at[dy, other(yl, dl), i], r_y2.at[n, i], along_y[n])
            for n, (dy, dl) in enumerate(y_steps)
        ]

    def to_sib(i):
        return send(part.at[i * 2 + 1], r_sib.at[i], sib)

    def on_chip(i, arrived):
        arrived.wait_recv()
        x_first[i] = (part[i * 2, 0].astype(F32) + r_sib[i, 0].astype(F32)).astype(BF)
        copy = send(x_first.at[i], r_x1.at[i // 2], along_x[i]) if i % 2 else None
        y_first[:, :, i] = (part[i * 2, 1].astype(F32) + r_sib[i, 1].astype(F32)).astype(BF)
        return copy, y_sends(i)

    def x_after_y(i, copies):
        a_2[i] = summed(y_first[0, yl, i].astype(F32), r_y2.at[:, i], copies).astype(BF)
        return send(a_2.at[i], r_x2.at[i - 1], along_x[i]) if i else None

    forward_sum()
    wv_sib = weight_terms(0, lift_t, do_v)
    forward_rest()
    unit(2, 1)
    sib_2 = to_sib(2)
    wv_x = weight_on_chip(0, wv_sib)
    unit(2, 0)
    unit(1, 1)
    sib_1 = to_sib(1)
    _, y_2 = on_chip(2, sib_2)
    paired = [
        send(x_first.at[2, 1 - parity, q], r_pair.at[q], to)
        for q, to in ((0, along_z[0]), (1, along_z[6]))
    ]
    unit(1, 0)
    unit(3, 1)
    sib_3 = to_sib(3)
    x_1, y_1 = on_chip(1, sib_1)
    for q, copy in enumerate(paired):
        copy.wait_recv()
        x_half[q] = (x_first[2, parity, q].astype(F32) + r_pair[q].astype(F32)).astype(BF)
    x_2 = send(x_half, r_half, along_x[2])
    unit(3, 0)
    unit(0, 1)
    sib_0 = to_sib(0)
    x_3, y_3 = on_chip(3, sib_3)
    unit(0, 0)
    _, y_0 = on_chip(0, sib_0)
    wv_y = weight_on_y(0, wv_x)
    x_sent = [x_after_y(2, y_2)]

    def query_lift_grads():
        for c in range(4):
            rows = slice(c * 512, (c + 1) * 512)
            add = dot(side_by_side(c * 4, 4, WIDTH), ed[rows, :STACK])
            if c == 0:
                dql[...] = add
            else:
                dql[...] += add
        lift_t[...] = (dql[:LATENT, :] * SCALE).astype(BF)

    query_lift_grads()
    wk_sib = weight_terms(1, lift_t, q_nope)

    def token_outputs():
        for h in range(HEADS_DEV):
            cols = slice(h * ROWS, (h + 1) * ROWS)
            dq_t[h * QK : h * QK + NOPE, :] = dot(wk_t[cols, :], lift_t[:, cols])
            dq_t[h * QK + NOPE : (h + 1) * QK, :] = dql[LATENT:, cols] * SCALE
        dq_ref[...] = dq_t[...].T.astype(BF)
        out_ref[...] = flip(o_t[...]).astype(BF)

    token_outputs()
    x_sent.insert(0, x_after_y(1, y_1))
    total = summed(x_first[0].astype(F32), r_x1, [x_1, x_3])
    x_2.wait_recv()
    for dy in range(2):
        half = jnp.where(parity == dy, r_half[...].astype(F32), 0.0)
        a_1[dy] = (total[dy] + half).astype(BF)
    y_sent = [
        send(a_1.at[dy, other(yl, dl)], r_y1.at[n], along_y[n])
        for n, (dy, dl) in enumerate(y_steps)
    ]
    x_sent.append(x_after_y(3, y_3))
    x_after_y(0, y_0)
    wk_x = weight_on_chip(1, wk_sib)

    def for_z(total, first):
        for n in range(4):
            piece = total[n * 8 : (n + 1) * 8]
            low = jnp.concatenate([piece[:, :256], piece[:, LATENT:]], axis=1)
            high = jnp.concatenate([piece[:, 256:LATENT], jnp.zeros((8, ROPE), F32)], axis=1)
            to_z[first + n] = jnp.concatenate([low, high], axis=0).astype(BF)

    for_z(summed(a_1[0, yl].astype(F32), r_y1, y_sent), 0)
    for_z(summed(a_2[0].astype(F32), r_x2, x_sent), 4)
    z_sent = [
        send(to_z.at[lax.rem(z + d, 8)], r_z.at[d - 1], along_z[d - 1]) for d in range(1, 8)
    ]
    wk_y = weight_on_y(1, wk_x)
    dwv_ref[...] = weight_end(0, wv_y)
    total = summed(to_z[z].astype(F32), r_z, z_sent)
    dlat_ref[:, :256] = total[:8, :256]
    dlat_ref[:, 256:LATENT] = total[8:, :256]
    dlat_ref[:, LATENT:] = total[:8, 256:]
    dwk_ref[...] = weight_end(1, wk_y)
    for copy in started:
        copy.wait_send()


COPIES = 72


def hand_on(*refs):
    held, targets, sem = refs[:5], refs[5:10], refs[10]
    copies = [
        pltpu.make_async_copy(src, dst, sem.at[n])
        for n, (src, dst) in enumerate(zip(held, targets))
    ]
    for copy in copies:
        copy.start()
    for copy in copies:
        copy.wait()


def on_device(latent, query, up_key, up_value, out_grad, block_pos):
    vmem = pltpu.VMEM
    shapes = (
        jax.ShapeDtypeStruct((ROWS, STACK), BF),
        jax.ShapeDtypeStruct((ROWS, HEADS_DEV * QK), BF),
        jax.ShapeDtypeStruct((8, WIDTH), F32),
        jax.ShapeDtypeStruct((32, STACK), F32),
        jax.ShapeDtypeStruct((32, STACK), F32),
    )
    scratch = [
        vmem((SEQ, WIDTH), BF),
        vmem((16, WIDTH, ROWS), BF),
        vmem((ROWS, HEADS_DEV * QK), BF),
        vmem((LATENT, STACK), BF),
        vmem((LATENT, STACK), BF),
        vmem((ROWS, STACK), BF),
        vmem((STACK, LATENT), BF),
        vmem((STACK, LATENT), BF),
        vmem((HEADS_DEV * QK, ROWS), BF),
        vmem((STACK, ROWS), BF),
        vmem((ROWS, STACK), BF),
        vmem((WIDTH, STACK), BF),
        vmem((2 * STACK, LATENT), BF),
        vmem((STACK, ROPE), BF),
        vmem((LATENT, STACK), F32),
        vmem((LATENT, STACK), BF),
        vmem((SEQ, STACK), F32),
        vmem((SEQ, 2 * STACK), BF),
        vmem((LATENT, STACK), F32),
        vmem((LATENT, STACK), BF),
        vmem((STACK, ROWS), BF),
        vmem((HEADS_DEV * QK, ROWS), F32),
        vmem((WIDTH, STACK), F32),
        vmem((8, STACK), F32),
        vmem((8, STACK), F32),
        vmem((1, STACK), F32),
        vmem((1, STACK), F32),
        vmem((1, STACK), F32),
        vmem((8, 2, 2, 2, 32, WIDTH), BF),
        vmem((4, 2, 2, 2, 32, WIDTH), BF),
        vmem((4, 2, 2, 32, WIDTH), BF),
        vmem((2, 2, 2, 32, WIDTH), BF),
        vmem((2, 32, WIDTH), BF),
        vmem((2, 32, WIDTH), BF),
        vmem((2, 32, WIDTH), BF),
        vmem((2, 2, 32, WIDTH), BF),
        vmem((3, 32, WIDTH), BF),
        vmem((2, 2, 4, 32, WIDTH), BF),
        vmem((3, 4, 32, WIDTH), BF),
        vmem((4, 32, WIDTH), BF),
        vmem((3, 32, WIDTH), BF),
        vmem((8, 16, 256 + ROPE), BF),
        vmem((7, 16, 256 + ROPE), BF),
        vmem((2, 2, 2, 4, 32, STACK), BF),
        vmem((2, 2, 4, 32, STACK), BF),
        vmem((2, 2, 4, 32, STACK), BF),
        vmem((2, 3, 2, 32, STACK), BF),
        vmem((2, 2, 32, STACK), BF),
        vmem((2, 32, STACK), BF),
    ]
    scratch += [
        pltpu.SemaphoreType.DMA((5,)),
        pltpu.SemaphoreType.REGULAR((2,)),
        pltpu.SemaphoreType.DMA((COPIES,)),
        pltpu.SemaphoreType.DMA((COPIES,)),
    ]
    hbm = pl.BlockSpec(memory_space=pl.ANY)
    in_vmem = pl.BlockSpec(memory_space=pltpu.VMEM)
    results = pl.pallas_call(
        kernel,
        out_shape=tuple(vmem(shape.shape, shape.dtype) for shape in shapes),
        in_specs=[hbm] * 5 + [pl.BlockSpec(memory_space=pltpu.SMEM)],
        out_specs=[in_vmem] * 5,
        scratch_shapes=scratch,
        compiler_params=pltpu.CompilerParams(
            collective_id=0, has_side_effects=True, vmem_limit_bytes=56 * 1024 * 1024
        ),
        cost_estimate=pl.CostEstimate(
            flops=7_000_000_000, bytes_accessed=4_000_000, transcendentals=1_048_576
        ),
    )(latent.T, query, up_key, up_value, out_grad, block_pos)
    return tuple(
        pl.pallas_call(
            hand_on,
            out_shape=shapes,
            in_specs=[in_vmem] * 5,
            out_specs=[hbm] * 5,
            scratch_shapes=[pltpu.SemaphoreType.DMA((5,))],
        )(*[pltpu.with_memory_space_constraint(r, pltpu.VMEM) for r in results])
    )


def solution(mesh):
    in_specs = (
        P("ctx", None),
        P("ctx", "head"),
        P(None, "head"),
        P(None, "head"),
        P("ctx", "head"),
        P(),
    )
    out_specs = (
        P("ctx", "head"),
        P("ctx", "head"),
        P(("ctx", "head"), None),
        P("ctx", "head"),
        P("ctx", "head"),
    )
    return jax.shard_map(
        on_device, mesh=mesh, in_specs=in_specs, out_specs=out_specs, check_vma=False
    )
```

```python
import functools
import math

import jax
import jax.numpy as jnp
from jax import lax
from jax.experimental import pallas as pl
from jax.experimental.pallas import tpu as pltpu
from jax.sharding import PartitionSpec as P

LATENT = 512
ROPE = 64
WIDTH = LATENT + ROPE
NOPE = 128
VDIM = 128
QK = NOPE + ROPE
ROWS = 128
HEADS_DEV = 4
STACK = HEADS_DEV * ROWS
SEQ = 2048
HALF = WIDTH // 2
SCALE = 1.0 / math.sqrt(QK)
LOG2E = 1.4426950408889634
MASKED = -1e30

BF = jnp.bfloat16
F32 = jnp.float32


def dot(a, b):
    return jnp.dot(a, b, preferred_element_type=F32)


def flip(a):
    return a.astype(F32).T


EARLY = 10


def slot(i, dk, dy):
    if i and dy:
        return EARLY + (i - 1) * 2 + dk
    return (dy if i == 0 else i + 1) * 2 + dk


def other(a, flip_it):
    return 1 - a if flip_it else a


def kernel(
    latent_t_hbm, query_hbm, wk_hbm, wv_hbm, dout_hbm, bpos,
    out_ref, dq_ref, dlat_ref, dwk_ref, dwv_ref,
    lat, lat_t, q_v, wk, wv, do_v, wk_t, wv_t, q_t, do_t, q_nope,
    qs_t, qd, q_rope, dlift, dos_t, scores, ed, lift_acc, lift_t, o_t, dq_t, dql,
    top, stats, rescale_row, inverse_row, delta_row, part, r_sib, x_first, r_x1, r_pair, x_half, r_half, a_1, r_y1, y_first, r_y2, a_2, r_x2,
    to_z, r_z, w_own, w_sib, w_acc, w_x, w_col, w_y, w_r,
    load_sem, ring_sem, send_sem, recv_sem,
):
    ctx, head = lax.axis_index("ctx"), lax.axis_index("head")
    x, yh, core = lax.div(ctx, 4), lax.rem(lax.div(ctx, 2), 2), lax.rem(ctx, 2)
    z, yl = lax.div(head, 2), lax.rem(head, 2)

    def x_at(i):
        return lax.rem(x + i, 4)

    def dev(i, dy, dk, dz, dl):
        xx, yy, kk = x_at(i), other(yh, dy), other(core, dk)
        return ((xx * 2 + yy) * 2 + kk, lax.rem(z + dz, 8) * 2 + other(yl, dl))

    sib = dev(0, 0, 1, 0, 0)
    near_y = dev(0, 1, 0, 0, 1)
    along_x = [None] + [dev(i, 0, 0, 0, 0) for i in range(1, 4)]
    y_steps = [(0, 1), (1, 0), (1, 1)]
    along_y = [dev(0, dy, 0, 0, dl) for dy, dl in y_steps]
    along_z = [dev(0, 0, 0, d, 0) for d in range(1, 8)]

    parity = lax.rem(z, 2)
    plane_steps = [(i, dy) for i in range(4) for dy in range(2)][1:]
    plane = [dev(i, dy, 0, 0, 0) for i, dy in plane_steps]

    loads = [
        pltpu.make_async_copy(src, dst, load_sem.at[n])
        for n, (src, dst) in enumerate(
            [
                (latent_t_hbm, lat_t.at[0]),
                (query_hbm, q_v),
                (wk_hbm, wk),
                (dout_hbm, do_v),
                (wv_hbm, wv),
            ]
        )
    ]
    for load in loads:
        load.start()

    barrier = pltpu.get_barrier_semaphore()
    partners = [sib] + along_x[1:] + along_y + [along_z[0], along_z[6]]
    for partner in partners:
        pl.semaphore_signal(barrier, inc=1, device_id=partner, device_id_type=pl.DeviceIdType.MESH)
    pl.semaphore_wait(barrier, len(partners))

    def greet(n, d):
        for to in (along_z[d - 1], along_z[7 - d]):
            pl.semaphore_signal(
                ring_sem.at[n], inc=1, device_id=to, device_id_type=pl.DeviceIdType.MESH
            )

    greet(0, 1)

    started = []

    def send(src, dst, to):
        n = len(started)
        assert n < COPIES
        copy = pltpu.make_async_remote_copy(
            src_ref=src, dst_ref=dst, send_sem=send_sem.at[n], recv_sem=recv_sem.at[n],
            device_id=to, device_id_type=pl.DeviceIdType.MESH,
        )
        copy.start()
        started.append(copy)
        return copy

    def block(i, dk, dy, h=None):
        if h is None:
            return lat_t.at[slot(i, dk, dy)]
        return lat_t.at[slot(i, dk, dy), pl.ds(pl.multiple_of(h * HALF, 16), HALF)]

    def send_halves(src, dst, to):
        return [send(block(*src, h), block(*dst, h), to) for h in range(2)]

    def trade_quarters(*where):
        copies = []
        for q, to in ((0, along_z[0]), (1, along_z[6])):
            rows = pl.ds(pl.multiple_of(parity * HALF + q * (HALF // 2), 16), HALF // 2)
            quarter = lat_t.at[slot(*where), rows]
            copies.append(send(quarter, quarter, to))
        return copies

    sib_got = {}

    def pass_on(i, dy, h=None):
        copy = send(block(i, 0, dy, h), block(i, 1, dy, h), sib)
        sib_got.setdefault((i, dy), []).append(copy)

    def passed(i, dy):
        for copy in sib_got[i, dy]:
            copy.wait_recv()

    loads[0].wait()
    from_x2 = send(block(0, 0, 0, parity), block(2, 0, 0, parity), along_x[2])
    from_y = send_halves((0, 0, 0), (0, 0, 1), near_y)
    pass_on(0, 0)

    for load in loads[1:]:
        load.wait()

    def lift_queries():
        q_t[...] = flip(q_v[...]).astype(BF)
        for h in range(HEADS_DEV):
            cols = slice(h * ROWS, (h + 1) * ROWS)
            q_h_t = q_t[h * QK : h * QK + NOPE, :]
            q_lift = dot(wk[:, cols], q_h_t)
            qs_t[:LATENT, cols] = (q_lift * (SCALE * LOG2E)).astype(BF)
            rope_t = q_t[h * QK + NOPE : (h + 1) * QK, :].astype(F32)
            qs_t[LATENT:, cols] = (rope_t * (SCALE * LOG2E)).astype(BF)

    from_x3 = send(block(0, 0, 0), block(3, 0, 0), along_x[1])
    from_x1 = send(block(0, 0, 0), block(1, 0, 0), along_x[3])
    lift_queries()
    query_row = lax.broadcasted_iota(jnp.int32, (1, STACK), 1)
    query_pos = (
        jnp.where(lax.rem(query_row, 128) < 64, bpos[2 * ctx], bpos[2 * ctx + 1]) * 64
        + lax.rem(query_row, 64)
    )
    top[...] = jnp.full(top.shape, MASKED, F32)
    key_row = lax.broadcasted_iota(jnp.int32, (ROWS, 1), 0)

    def score_block(i, dk, dy):
        rows = pl.ds(slot(i, dk, dy) * ROWS, ROWS)
        owner = (x_at(i) * 2 + other(yh, dy)) * 2 + other(core, dk)
        keys = flip(lat_t[slot(i, dk, dy)]).astype(BF)
        lat[rows, :] = keys
        key_pos = (
            jnp.where(key_row < 64, bpos[2 * owner], bpos[2 * owner + 1]) * 64
            + lax.rem(key_row, 64)
        )
        s = jnp.where(key_pos <= query_pos, dot(keys, qs_t[...]), MASKED)
        scores[rows, :] = s
        top[...] = jnp.maximum(top[...], jnp.max(s.reshape(ROWS // 8, 8, STACK), axis=0))

    score_block(0, 0, 0)
    pl.semaphore_wait(ring_sem.at[0], 2)
    greet(1, 2)
    up_x3, up_x1 = [], []

    def up_x(h):
        from_y[h].wait_recv()
        up_x3.append(send(block(0, 0, 1, h), block(3, 0, 1, h), along_x[1]))
        up_x1.append(send(block(0, 0, 1, h), block(1, 0, 1, h), along_x[3]))

    up_x(0)
    from_x2.wait_recv()
    up_y = [send(block(2, 0, 0, parity), block(2, 0, 1, parity), near_y)]
    traded = trade_quarters(2, 0, 0)
    up_x(1)
    pass_on(0, 1)
    passed(0, 0)
    score_block(0, 1, 0)
    from_x3.wait_recv()
    pass_on(3, 0)
    from_x1.wait_recv()
    pass_on(1, 0)
    score_block(0, 0, 1)
    for copy in traded:
        copy.wait_recv()
    up_y.append(send(block(2, 0, 0, 1 - parity), block(2, 0, 1, 1 - parity), near_y))
    pass_on(2, 0)
    score_block(3, 0, 0)
    score_block(1, 0, 0)

    def lift_rest():
        wk_t[...] = flip(wk[...]).astype(BF)
        wv_t[...] = flip(wv[...]).astype(BF)
        do_t[...] = flip(do_v[...]).astype(BF)
        for h in range(HEADS_DEV):
            cols = slice(h * ROWS, (h + 1) * ROWS)
            q_nope[:, cols] = flip(q_t[h * QK : h * QK + NOPE, :]).astype(BF)
            rope = flip(q_t[h * QK + NOPE : (h + 1) * QK, :])
            q_rope[cols, :] = (rope * SCALE).astype(BF)
            qd[cols, :] = (dot(q_nope[:, cols], wk_t[cols, :]) * SCALE).astype(BF)
            dlift[:, cols] = dot(wv[:, cols], do_t[cols, :])

    lift_rest()
    pl.semaphore_wait(ring_sem.at[1], 2)
    passed(0, 1)
    score_block(0, 1, 1)
    score_block(2, 0, 0)
    passed(3, 0)
    score_block(3, 1, 0)
    passed(1, 0)
    score_block(1, 1, 0)
    passed(2, 0)
    score_block(2, 1, 0)

    def side_by_side(first, count, width):
        return jnp.concatenate(
            [lat_t[first + n, :width, :] for n in range(count)], axis=1
        )

    def exponentials(first, last, row_max):
        total = jnp.zeros((8, STACK), F32)
        for start in range(first, last, 4):
            count = min(4, last - start)
            rows = slice(start * ROWS, (start + count) * ROWS)
            e = jnp.exp2(scores[rows, :] - row_max)
            total = total + jnp.sum(e.reshape(count * ROWS // 8, 8, STACK), axis=0)
            ed[rows, STACK:] = e.astype(BF)
            add = dot(side_by_side(start, count, LATENT), ed[rows, STACK:])
            if start == 0:
                lift_acc[...] = add
            else:
                lift_acc[...] += add
        return jnp.sum(total, axis=0, keepdims=True)

    def forward_early():
        early_max = jnp.max(top[...], axis=0, keepdims=True)
        stats[0:1, :] = early_max
        stats[1:2, :] = exponentials(0, EARLY, early_max)

    def forward_sum():
        early_max = stats[0:1, :]
        row_max = jnp.max(top[...], axis=0, keepdims=True)
        rescale = jnp.exp2(early_max - row_max)
        rescale_row[...] = rescale
        lift_acc[...] = lift_acc[...] * rescale
        total = stats[1:2, :] * rescale + exponentials(EARLY, 16, row_max)
        inverse = 1.0 / total
        lift_t[...] = (lift_acc[...] * inverse).astype(BF)
        inverse_row[...] = inverse

    def forward_rest():
        inverse = inverse_row[...]
        deltas = []
        for h in range(HEADS_DEV):
            cols = slice(h * ROWS, (h + 1) * ROWS)
            o_low = dot(wv_t[cols, :], lift_t[:, cols]).astype(BF)
            o_t[cols, :] = o_low
            deltas.append(
                jnp.sum(do_t[cols, :].astype(F32) * o_low.astype(F32), axis=0, keepdims=True)
            )
            scaled = dlift[:, cols] * inverse[:, cols]
            dos_t[:, cols] = scaled.astype(BF)
            qd[STACK + h * ROWS : STACK + (h + 1) * ROWS, :] = scaled.T.astype(BF)
        delta_row[...] = jnp.concatenate(deltas, axis=1) * inverse

    forward_early()
    for h, y_half in ((0, parity), (1, 1 - parity)):
        up_x3[h].wait_recv()
        pass_on(3, 1, h)
        up_x1[h].wait_recv()
        pass_on(1, 1, h)
        up_y[h].wait_recv()
        pass_on(2, 1, y_half)
    score_block(3, 0, 1)
    score_block(1, 0, 1)
    score_block(2, 0, 1)
    passed(3, 1)
    score_block(3, 1, 1)
    passed(1, 1)
    score_block(1, 1, 1)
    passed(2, 1)
    score_block(2, 1, 1)

    def weight_terms(n, lifted, by):
        for h in range(HEADS_DEV):
            cols = slice(h * ROWS, (h + 1) * ROWS)
            g = dot(lifted[:, cols], by[:, cols]).astype(BF)
            for piece in range(16):
                xx, yy, kk = piece // 4, piece // 2 % 2, piece % 2
                w_own[n, kk, yy, xx, :, cols] = g[piece * 32 : (piece + 1) * 32, :]
        return send(w_own.at[n, 1 - core], w_sib.at[n], sib)

    def weight_on_chip(n, arrived):
        arrived.wait_recv()
        w_acc[n] = (w_own[n, core].astype(F32) + w_sib[n].astype(F32)).astype(BF)

    def weight_on_x(n):
        return [send(w_acc.at[n, :, x_at(i)], w_x.at[i - 1], along_x[i]) for i in range(1, 4)]

    def weight_on_y(n, arrived):
        w_col[...] = summed(w_acc[n, :, x].astype(F32), w_x, arrived).astype(BF)
        return send(w_col.at[1 - yh], w_y, along_y[1])

    def weight_direct(n):
        return [
            send(w_acc.at[n, other(yh, dy), x_at(i)], w_r.at[m], plane[m])
            for m, (i, dy) in enumerate(plane_steps)
        ]

    def summed(total, ref, arrived):
        for n, copy in enumerate(arrived):
            copy.wait_recv()
            total = total + ref[n].astype(F32)
        return total

    def unit(i, dk):
        u = i * 2 + dk
        spans = [pl.ds(slot(i, dk, dy) * ROWS, ROWS) for dy in range(2)]

        def both(ref, cols):
            return jnp.concatenate([ref[rows, cols] for rows in spans], axis=0)

        dp = dot(both(lat, slice(0, LATENT)), dos_t[...])
        for dy, rows in enumerate(spans):
            e = ed[rows, STACK:].astype(F32)
            if slot(i, dk, dy) < EARLY:
                e = e * rescale_row[...]
                ed[rows, STACK:] = e.astype(BF)
            ds = e * (dp[dy * ROWS : (dy + 1) * ROWS] - delta_row[...])
            ed[rows, :STACK] = ds.astype(BF)
        nope = dot(both(ed, slice(None)), qd[...])
        rope = dot(both(ed, slice(0, STACK)), q_rope[...])
        for half in range(2):
            for dy in range(2):
                for low in range(2):
                    starts = [dy * 128 + half * 64 + n * 16 + low * 8 for n in range(4)]
                    part[u, half, dy, low, :, :LATENT] = jnp.concatenate(
                        [nope[r : r + 8, :] for r in starts], axis=0
                    ).astype(BF)
                    part[u, half, dy, low, :, LATENT:] = jnp.concatenate(
                        [rope[r : r + 8, :] for r in starts], axis=0
                    ).astype(BF)

    def y_sends(i):
        return [
            send(y_first.at[dy, other(yl, dl), i], r_y2.at[n, i], along_y[n])
            for n, (dy, dl) in enumerate(y_steps)
        ]

    def to_sib(i):
        return send(part.at[i * 2 + 1], r_sib.at[i], sib)

    def on_chip(i, arrived):
        arrived.wait_recv()
        x_first[i] = (part[i * 2, 0].astype(F32) + r_sib[i, 0].astype(F32)).astype(BF)
        copy = send(x_first.at[i], r_x1.at[i // 2], along_x[i]) if i % 2 else None
        y_first[:, :, i] = (part[i * 2, 1].astype(F32) + r_sib[i, 1].astype(F32)).astype(BF)
        return copy, y_sends(i)

    def x_after_y(i, copies):
        a_2[i] = summed(y_first[0, yl, i].astype(F32), r_y2.at[:, i], copies).astype(BF)
        return send(a_2.at[i], r_x2.at[i - 1], along_x[i]) if i else None

    forward_sum()
    wv_sib = weight_terms(0, lift_t, do_v)
    forward_rest()
    unit(2, 1)
    sib_2 = to_sib(2)
    weight_on_chip(0, wv_sib)
    wv_x = weight_on_x(0)
    unit(2, 0)
    unit(1, 1)
    sib_1 = to_sib(1)
    _, y_2 = on_chip(2, sib_2)
    paired = [
        send(x_first.at[2, 1 - parity, q], r_pair.at[q], to)
        for q, to in ((0, along_z[0]), (1, along_z[6]))
    ]
    unit(1, 0)
    unit(3, 1)
    sib_3 = to_sib(3)
    x_1, y_1 = on_chip(1, sib_1)
    for q, copy in enumerate(paired):
        copy.wait_recv()
        x_half[q] = (x_first[2, parity, q].astype(F32) + r_pair[q].astype(F32)).astype(BF)
    x_2 = send(x_half, r_half, along_x[2])
    unit(3, 0)
    unit(0, 1)
    sib_0 = to_sib(0)
    x_3, y_3 = on_chip(3, sib_3)
    unit(0, 0)
    _, y_0 = on_chip(0, sib_0)
    wv_y = weight_on_y(0, wv_x)
    x_sent = [x_after_y(2, y_2)]

    def query_lift_grads():
        for c in range(4):
            rows = slice(c * 512, (c + 1) * 512)
            add = dot(side_by_side(c * 4, 4, WIDTH), ed[rows, :STACK])
            if c == 0:
                dql[...] = add
            else:
                dql[...] += add
        lift_t[...] = (dql[:LATENT, :] * SCALE).astype(BF)

    query_lift_grads()
    wk_sib = weight_terms(1, lift_t, q_nope)

    def token_outputs():
        for h in range(HEADS_DEV):
            cols = slice(h * ROWS, (h + 1) * ROWS)
            dq_t[h * QK : h * QK + NOPE, :] = dot(wk_t[cols, :], lift_t[:, cols])
            dq_t[h * QK + NOPE : (h + 1) * QK, :] = dql[LATENT:, cols] * SCALE
        dq_ref[...] = dq_t[...].T.astype(BF)
        out_ref[...] = flip(o_t[...]).astype(BF)

    token_outputs()
    x_sent.insert(0, x_after_y(1, y_1))
    total = summed(x_first[0].astype(F32), r_x1, [x_1, x_3])
    x_2.wait_recv()
    for dy in range(2):
        half = jnp.where(parity == dy, r_half[...].astype(F32), 0.0)
        a_1[dy] = (total[dy] + half).astype(BF)
    y_sent = [
        send(a_1.at[dy, other(yl, dl)], r_y1.at[n], along_y[n])
        for n, (dy, dl) in enumerate(y_steps)
    ]
    x_sent.append(x_after_y(3, y_3))
    x_after_y(0, y_0)
    weight_on_chip(1, wk_sib)
    wk_got = weight_direct(1)

    def for_z(total, first):
        for n in range(4):
            piece = total[n * 8 : (n + 1) * 8]
            low = jnp.concatenate([piece[:, :256], piece[:, LATENT:]], axis=1)
            high = jnp.concatenate([piece[:, 256:LATENT], jnp.zeros((8, ROPE), F32)], axis=1)
            to_z[first + n] = jnp.concatenate([low, high], axis=0).astype(BF)

    for_z(summed(a_1[0, yl].astype(F32), r_y1, y_sent), 0)
    for_z(summed(a_2[0].astype(F32), r_x2, x_sent), 4)
    z_sent = [
        send(to_z.at[lax.rem(z + d, 8)], r_z.at[d - 1], along_z[d - 1]) for d in range(1, 8)
    ]
    wv_y.wait_recv()
    dwv_ref[...] = w_col[yh].astype(F32) + w_y[...].astype(F32)
    total = summed(to_z[z].astype(F32), r_z, z_sent)
    dlat_ref[:, :256] = total[:8, :256]
    dlat_ref[:, 256:LATENT] = total[8:, :256]
    dlat_ref[:, LATENT:] = total[:8, 256:]
    dwk_ref[...] = summed(w_acc[1, yh, x].astype(F32), w_r, wk_got)
    for copy in started:
        copy.wait_send()


COPIES = 80


def hand_on(*refs):
    held, targets, sem = refs[:5], refs[5:10], refs[10]
    copies = [
        pltpu.make_async_copy(src, dst, sem.at[n])
        for n, (src, dst) in enumerate(zip(held, targets))
    ]
    for copy in copies:
        copy.start()
    for copy in copies:
        copy.wait()


def on_device(latent, query, up_key, up_value, out_grad, block_pos):
    vmem = pltpu.VMEM
    shapes = (
        jax.ShapeDtypeStruct((ROWS, STACK), BF),
        jax.ShapeDtypeStruct((ROWS, HEADS_DEV * QK), BF),
        jax.ShapeDtypeStruct((8, WIDTH), F32),
        jax.ShapeDtypeStruct((32, STACK), F32),
        jax.ShapeDtypeStruct((32, STACK), F32),
    )
    scratch = [
        vmem((SEQ, WIDTH), BF),
        vmem((16, WIDTH, ROWS), BF),
        vmem((ROWS, HEADS_DEV * QK), BF),
        vmem((LATENT, STACK), BF),
        vmem((LATENT, STACK), BF),
        vmem((ROWS, STACK), BF),
        vmem((STACK, LATENT), BF),
        vmem((STACK, LATENT), BF),
        vmem((HEADS_DEV * QK, ROWS), BF),
        vmem((STACK, ROWS), BF),
        vmem((ROWS, STACK), BF),
        vmem((WIDTH, STACK), BF),
        vmem((2 * STACK, LATENT), BF),
        vmem((STACK, ROPE), BF),
        vmem((LATENT, STACK), F32),
        vmem((LATENT, STACK), BF),
        vmem((SEQ, STACK), F32),
        vmem((SEQ, 2 * STACK), BF),
        vmem((LATENT, STACK), F32),
        vmem((LATENT, STACK), BF),
        vmem((STACK, ROWS), BF),
        vmem((HEADS_DEV * QK, ROWS), F32),
        vmem((WIDTH, STACK), F32),
        vmem((8, STACK), F32),
        vmem((8, STACK), F32),
        vmem((1, STACK), F32),
        vmem((1, STACK), F32),
        vmem((1, STACK), F32),
        vmem((8, 2, 2, 2, 32, WIDTH), BF),
        vmem((4, 2, 2, 2, 32, WIDTH), BF),
        vmem((4, 2, 2, 32, WIDTH), BF),
        vmem((2, 2, 2, 32, WIDTH), BF),
        vmem((2, 32, WIDTH), BF),
        vmem((2, 32, WIDTH), BF),
        vmem((2, 32, WIDTH), BF),
        vmem((2, 2, 32, WIDTH), BF),
        vmem((3, 32, WIDTH), BF),
        vmem((2, 2, 4, 32, WIDTH), BF),
        vmem((3, 4, 32, WIDTH), BF),
        vmem((4, 32, WIDTH), BF),
        vmem((3, 32, WIDTH), BF),
        vmem((8, 16, 256 + ROPE), BF),
        vmem((7, 16, 256 + ROPE), BF),
        vmem((2, 2, 2, 4, 32, STACK), BF),
        vmem((2, 2, 4, 32, STACK), BF),
        vmem((2, 2, 4, 32, STACK), BF),
        vmem((3, 2, 32, STACK), BF),
        vmem((2, 32, STACK), BF),
        vmem((32, STACK), BF),
        vmem((7, 32, STACK), BF),
    ]
    scratch += [
        pltpu.SemaphoreType.DMA((5,)),
        pltpu.SemaphoreType.REGULAR((2,)),
        pltpu.SemaphoreType.DMA((COPIES,)),
        pltpu.SemaphoreType.DMA((COPIES,)),
    ]
    hbm = pl.BlockSpec(memory_space=pl.ANY)
    in_vmem = pl.BlockSpec(memory_space=pltpu.VMEM)
    results = pl.pallas_call(
        kernel,
        out_shape=tuple(vmem(shape.shape, shape.dtype) for shape in shapes),
        in_specs=[hbm] * 5 + [pl.BlockSpec(memory_space=pltpu.SMEM)],
        out_specs=[in_vmem] * 5,
        scratch_shapes=scratch,
        compiler_params=pltpu.CompilerParams(
            collective_id=0, has_side_effects=True, vmem_limit_bytes=56 * 1024 * 1024
        ),
        cost_estimate=pl.CostEstimate(
            flops=7_000_000_000, bytes_accessed=4_000_000, transcendentals=1_048_576
        ),
    )(latent.T, query, up_key, up_value, out_grad, block_pos)
    return tuple(
        pl.pallas_call(
            hand_on,
            out_shape=shapes,
            in_specs=[in_vmem] * 5,
            out_specs=[hbm] * 5,
            scratch_shapes=[pltpu.SemaphoreType.DMA((5,))],
        )(*[pltpu.with_memory_space_constraint(r, pltpu.VMEM) for r in results])
    )


def solution(mesh):
    in_specs = (
        P("ctx", None),
        P("ctx", "head"),
        P(None, "head"),
        P(None, "head"),
        P("ctx", "head"),
        P(),
    )
    out_specs = (
        P("ctx", "head"),
        P("ctx", "head"),
        P(("ctx", "head"), None),
        P("ctx", "head"),
        P("ctx", "head"),
    )
    return jax.shard_map(
        on_device, mesh=mesh, in_specs=in_specs, out_specs=out_specs, check_vma=False
    )
```
